32 devices in a mesh: section: 4 (over y, x), dp: 2 (over core), expert: 4 (over z).
Axes of the slice: x: 2, y: 2, z: 4, core: 2. Of those that a mesh axis runs over, the one named last changes fastest.
Arguments:
- init_state: bfloat16 [4, 256, 5280], P(None, ('dp', 'expert')), may hold values from -5 to 5
- inject: bfloat16 [4, 256, 5280], P(None, ('dp', 'expert')), may hold values from -24 to 24
- routes: int32 [2, 4, 4, 256, 1], P(None, 'section', None, ('dp', 'expert')), may hold values from 0 to 3; in each aligned block of 32 rows (0 to 31, 32 to 63, ..., all dimensions but the last counted through in order) at most 12 rows name the same one
- norm_gain: float32 [4, 5280], P('section'), may hold values from 0.25 to 1.75
- router: bfloat16 [4, 4, 5280], P('section'), may hold values from -0.078125 to 0.078125
- w_up: bfloat16 [4, 4, 5280, 768], P('section', 'expert', 'dp'), may hold values from -0.078125 to 0.078125
- w_down: bfloat16 [4, 4, 768, 5280], P('section', 'expert', None, 'dp'), may hold values from -0.21875 to 0.21875
Outputs:
- final_state: bfloat16 [4, 256, 5280], P('section', ('dp', 'expert'))
The draws below stay inside these ranges and needn't reach their ends.
Inputs may be any that keep to these rules, and one draw needn't show every extreme that they name: In each aligned block of 32 tokens of routes, no expert is named by more than 12 tokens.
All inputs are finite; a program needn't handle non-finite values.
Results may differ from the reference program's by a relative error of at most 0.014.
Values may be sent and summed in bfloat16 or wider, within the bound.
No kernel may reach another device: no remote copies, remote signals or barrier semaphores. Data moves between devices by JAX's collectives and lax.ppermute only.
A program may use at most 128 MiB of HBM per device.

```python
import math
import jax
import jax.numpy as jnp
import numpy as np
from jax import lax

D = 5280
F = 768
TOK_DEV = 32
RECUR = 2
CAP = 12
EXPERTS = 4
MICRO = 4
MBT = 256
N_SECTION = 4
N_DP = 2
N_EXPERT = 4


def draw_inject(key, part):
    streams = jax.random.split(key, 3)
    extent = (MICRO, MBT, D)
    values = jnp.clip(jax.random.normal(streams[0], extent, jnp.float32), -4.0, 4.0)
    lowest = math.log(0.5)
    highest = math.log(2.0)
    row_scale = jnp.exp(jax.random.uniform(streams[1], (MICRO, MBT, 1), jnp.float32, lowest, highest))
    col_scale = jnp.exp(jax.random.uniform(streams[2], (1, 1, D), jnp.float32, lowest, highest))
    return (values * row_scale * col_scale).astype(jnp.bfloat16)


def shard_levels(stream_key, dims, shards, low, top_value):
    def one(axis_at, shards_of):
        steps = jax.random.uniform(jax.random.fold_in(jax.random.fold_in(stream_key, 6), axis_at), (shards_of,), jnp.float32, low / len(shards), top_value / len(shards))
        return jnp.repeat(jnp.exp(steps), dims[axis_at] // shards_of).reshape((-1,) + (1,) * (len(dims) - axis_at - 1))

    loudness = one(*shards[0])
    for cut in shards[1:]:
        loudness = loudness * one(*cut)
    return loudness


def shared_out(key, own, number, rows, count, top, reach, skew):
    sequence = jax.random.permutation(key, count)
    heavy_load, common = shares(count, rows * top, reach, skew, True), shares(count, rows * top, reach, skew, False)
    places = jnp.arange(count)

    def named(sizes, rotation):
        used = int((sizes > 0).sum())
        fixed = max(1, used // 4)
        moved = fixed + (places - fixed + rotation * (used - fixed)) % max(1, count - fixed)
        return jnp.zeros((count,), jnp.int32).at[sequence[jnp.where(places < fixed, places, moved)]].set(jnp.asarray(sizes, jnp.int32))

    sizes = jnp.where(number % 4 == 0, named(heavy_load, number // 4), named(common, number - number // 4 - 1))
    mixed = jax.random.permutation(jax.random.fold_in(own, 3), count)
    source_of, receiver = mixed[0:count // 2 * 2:2], mixed[1:count // 2 * 2:2]
    slack = jnp.minimum(sizes[source_of] - 1, reach - sizes[receiver]) // 2
    slack = jnp.where((source_of == sequence[0]) | (receiver == sequence[0]) | (sizes[receiver] == 0), 0, jnp.maximum(slack, 0))
    moved = jax.random.randint(jax.random.fold_in(own, 4), (count // 2,), 0, 1 << 20) % (slack + 1)
    sizes = sizes.at[source_of].add(-moved).at[receiver].add(moved)
    members = jnp.searchsorted(jnp.cumsum(sizes), jnp.arange(rows * top), side="right").astype(jnp.int32)
    listing = members.reshape(top, rows).T
    listing = listing[jax.random.permutation(jax.random.fold_in(own, 1), rows)]
    rotation = jax.random.randint(jax.random.fold_in(own, 2), (rows, 1), 0, top)
    return jnp.take_along_axis(listing, (jnp.arange(top)[None, :] + rotation) % top, axis=1)


def shares(number_of, total, limit, lean, full):
    portions = [(1 << 20) // math.isqrt(rank ** lean) + 1 for rank in range(1, number_of + 1)]
    largest = limit if full else min(limit, max(-(-total // number_of), total * portions[0] // sum(portions)))
    least = 1 if total - largest >= number_of - 1 else 0
    counts, spare = [largest] + [least] * (number_of - 1), total - largest - least * (number_of - 1)
    while spare > 0:
        free = [i for i in range(1, number_of) if counts[i] < largest] or [i for i in range(1, number_of) if counts[i] < limit]
        mass, budget = sum([portions[i] for i in free]), spare
        for i in free:
            addition = min(limit - counts[i], max(1, budget * portions[i] // mass), spare)
            counts[i] = counts[i] + addition
            spare = spare - addition
    return np.array(counts)


def bell_draw(own_key, shape, deviation, bound, cuts=(), held_as=jnp.bfloat16):
    drawn = deviation * jax.random.normal(own_key, shape, jnp.float32)
    if cuts:
        drawn = drawn * shard_levels(own_key, shape, cuts, -0.22, 0.18)
    return jnp.clip(drawn, -bound, bound).astype(held_as)


def setup_inputs(seed: int = 0) -> dict:
    key_list = jax.random.split(jax.random.key(seed), 8)
    init_state = bell_draw(key_list[0], (MICRO, MBT, D), 1.0, 5.0, ((1, 8),))
    inject = draw_inject(jax.random.fold_in(key_list[7], 71), 0)
    routes_keys = jax.random.split(jax.random.fold_in(key_list[2], 1), RECUR * N_SECTION * MICRO * MBT // TOK_DEV)
    routes_turns = jax.random.permutation(jax.random.fold_in(key_list[2], 3), RECUR * N_SECTION * MICRO * MBT // TOK_DEV)
    routes = jax.vmap(lambda own, number: shared_out(jax.random.fold_in(key_list[2], 2), own, number, TOK_DEV, EXPERTS, 1, CAP, 1))(routes_keys, routes_turns).reshape((RECUR, N_SECTION, MICRO, MBT, 1))
    norm_gain = jnp.clip(1.0 + 0.15 * jax.random.normal(key_list[3], (N_SECTION, D), jnp.float32), 0.25, 1.75)
    router = bell_draw(key_list[4], (N_SECTION, EXPERTS, D), D ** -0.5, 0.078125, ((0, 4),))
    w_up = bell_draw(key_list[5], (N_SECTION, EXPERTS, D, F), D ** -0.5, 0.078125, ((0, 4), (1, 4), (2, 2)))
    w_down = bell_draw(key_list[6], (N_SECTION, EXPERTS, F, D), F ** -0.5, 0.21875, ((0, 4), (1, 4), (3, 2)))
    return {"init_state": init_state, "inject": inject, "routes": routes, "norm_gain": norm_gain, "router": router, "w_up": w_up, "w_down": w_down}


def core_block(current, gain_row, router_rows, up_stack, down_stack, assign):
    as_float = current.astype(jnp.float32)
    inv_rms = lax.rsqrt(lax.optimization_barrier(jnp.mean(as_float * as_float, axis=-1, keepdims=True)) + 1e-05)
    normed = (as_float * inv_rms * gain_row).astype(jnp.bfloat16)
    logits = jnp.dot(normed, router_rows.T, preferred_element_type=jnp.float32)
    labels = jnp.arange(EXPERTS, dtype=jnp.int32)
    member = assign[:, None] == labels[None, :]
    gate_value = jax.nn.sigmoid(lax.optimization_barrier(jnp.sum(jnp.where(member, logits, jnp.float32(0.0)), axis=-1)))
    row_limit = N_DP * N_EXPERT * CAP
    collected = jnp.zeros(as_float.shape, jnp.float32)
    for expert_id in range(EXPERTS):
        chosen_mask = assign == expert_id
        chosen = jnp.nonzero(chosen_mask, size=row_limit, fill_value=0)[0].astype(jnp.int32)
        is_valid = jnp.arange(row_limit, dtype=jnp.int32) < jnp.sum(chosen_mask.astype(jnp.int32))
        picked_rows = normed[chosen]
        hidden = jax.nn.gelu(jnp.dot(picked_rows, up_stack[expert_id], preferred_element_type=jnp.float32)).astype(jnp.bfloat16)
        expert_out = jnp.dot(hidden, down_stack[expert_id], preferred_element_type=jnp.float32).astype(jnp.bfloat16)
        collected = collected.at[chosen].add(jnp.where(is_valid[:, None], expert_out.astype(jnp.float32), jnp.float32(0.0)))
    return (as_float + gate_value[:, None] * collected).astype(jnp.bfloat16)

def reference(init_state, inject, routes, norm_gain, router, w_up, w_down):
    finals = []
    for micro_idx in range(MICRO):
        current = (init_state[micro_idx].astype(jnp.float32) + inject[micro_idx].astype(jnp.float32)).astype(jnp.bfloat16)
        for round_idx in range(RECUR):
            if round_idx > 0:
                current = (current.astype(jnp.float32) + inject[micro_idx].astype(jnp.float32)).astype(jnp.bfloat16)
            for block_idx in range(N_SECTION):
                current = core_block(current, norm_gain[block_idx], router[block_idx], w_up[block_idx], w_down[block_idx], routes[round_idx, block_idx, micro_idx, :, 0])
        finals.append(current)
    return jnp.stack(finals)
```

```python
import functools
import jax
import jax.numpy as jnp
import numpy as np
from jax import lax
from jax.experimental import pallas as pl
from jax.experimental.pallas import tpu as pltpu
from jax.sharding import PartitionSpec as P

RECUR = 2
CAP = 12
SAME_CAP = 20
OTHER_CAP = 16
SPARE_CAP = 4
META = 16
HOME = 8
EPS = 1e-05
VMEM_LIMIT = 16 << 20
BF = jnp.bfloat16
F32 = jnp.float32
JOINT = ("section", "expert")


def shifted(block, axis, distance):
    devices = range(lax.axis_size(axis))
    route = [((i - distance) % len(devices), i) for i in devices]
    return lax.ppermute(block, axis, route)


def normalize(current, gain_row):
    as_float = current.astype(F32)
    inv_rms = lax.rsqrt(jnp.mean(as_float * as_float, axis=-1, keepdims=True) + EPS)
    return (as_float * inv_rms * gain_row).astype(BF)


def expert_rows(item_rows, w_first, w_second):
    extent = item_rows.shape
    flat_rows = item_rows.reshape(-1, extent[-1])
    hidden = jax.nn.gelu(jnp.dot(flat_rows, w_first, preferred_element_type=F32)).astype(BF)
    result = jnp.dot(hidden, w_second, preferred_element_type=F32).astype(BF)
    return result.reshape(extent)


def whole_round(buffer, w_first, w_second):
    processed = expert_rows(
        lax.all_to_all(buffer, "expert", split_axis=0, concat_axis=0, tiled=True), w_first, w_second
    )
    return lax.all_to_all(processed, "expert", split_axis=0, concat_axis=0, tiled=True)


def core_block(current, gain_row, router_rows, w_first, w_second, assign):
    tokens = current.shape[0]
    experts = router_rows.shape[0]
    normed = normalize(current, gain_row)
    logits = jnp.dot(normed, router_rows.T, preferred_element_type=F32)
    labels = lax.broadcasted_iota(jnp.int32, (tokens, experts), 1)
    onehot = (assign[:, None] == labels).astype(F32)
    gate_value = jax.nn.sigmoid(jnp.sum(onehot * logits, axis=-1))
    earlier = (
        lax.broadcasted_iota(jnp.int32, (tokens, tokens), 0)
        > lax.broadcasted_iota(jnp.int32, (tokens, tokens), 1)
    ).astype(F32)
    counts = jnp.dot(earlier, onehot, preferred_element_type=F32)
    slot_index = jnp.sum(onehot * counts, axis=-1).astype(jnp.int32)
    target = assign * CAP + slot_index
    places = (
        lax.broadcasted_iota(jnp.int32, (experts * CAP, tokens), 0) == target[None, :]
    ).astype(BF)
    buffer = (
        jnp.dot(places, normed, preferred_element_type=F32).astype(BF).reshape(experts, CAP, -1)
    )
    returned = whole_round(buffer, w_first, w_second)
    flat_back = returned.reshape(experts * CAP, -1)
    expert_out = jnp.einsum("st,sd->td", places, flat_back, preferred_element_type=F32)
    updated = current.astype(F32) + gate_value[:, None] * expert_out
    return updated.astype(BF)


def general_body(init_state, inject, routes, norm_gain, router, w_up, w_down):
    sections = lax.axis_size("section")
    section_index = lax.axis_index("section")
    w_first = lax.all_gather(w_up, "dp", axis=2, tiled=True)[0, 0]
    w_second = lax.all_gather(w_down, "dp", axis=3, tiled=True)[0, 0]
    gain_row = norm_gain[0]
    router_rows = router[0]
    tokens = init_state.shape[1]
    active_span = sections * RECUR
    total_steps = active_span + sections - 1

    def advance(moment, hidden_state):
        offset = moment - section_index
        is_live = (offset >= 0) & (offset < active_span)
        clipped = jnp.clip(offset, 0, active_span - 1)
        loop_round = clipped // sections
        entry_slot = clipped % sections
        micro_idx = jnp.mod(sections - 2 - entry_slot, sections)
        initial = lax.dynamic_index_in_dim(init_state, micro_idx, 0, keepdims=False)
        injected_row = lax.dynamic_index_in_dim(inject, micro_idx, 0, keepdims=False)
        incoming = jnp.where(loop_round == 0, initial, hidden_state)
        injected = (incoming.astype(F32) + injected_row.astype(F32)).astype(BF)
        entering = is_live & (section_index == 0)
        current = jnp.where(entering, injected, hidden_state)
        assign = lax.dynamic_slice(
            routes, (loop_round, 0, micro_idx, 0, 0), (1, 1, 1, tokens, 1)
        ).reshape(tokens)
        result = core_block(current, gain_row, router_rows, w_first, w_second, assign)
        return jnp.where(is_live, result, hidden_state)

    def advance_one(moment, hidden_state):
        return advance(moment, shifted(hidden_state, "section", 1))

    hidden_state = jnp.zeros(init_state.shape[1:], BF)
    hidden_state = advance(0, hidden_state)
    hidden_state = lax.fori_loop(1, total_steps, advance_one, hidden_state)
    return hidden_state[None]


def rows_of(refs):
    return jnp.concatenate([r[...].astype(F32) for r in refs], axis=0)


def column(block, index):
    lanes = lax.broadcasted_iota(jnp.int32, block.shape, 1)
    return jnp.sum(jnp.where(lanes == index, block, 0.0), axis=1, keepdims=True)


def places_of(meta, at, next_idx, own, sizes, experts, ident):
    same, other = sizes[0], sizes[1]
    spare = sizes[experts] // (experts - 1) if len(sizes) > experts else 0
    main = same + (experts - 1) * other
    rows = meta.shape[0]
    dest = column(meta, at + next_idx)
    lanes = lax.broadcasted_iota(jnp.int32, meta.shape, 1)
    onehot = (((lanes + 1).astype(F32) == dest) & (lanes < experts)).astype(F32)
    earlier = (
        lax.broadcasted_iota(jnp.int32, (rows, rows), 0)
        > lax.broadcasted_iota(jnp.int32, (rows, rows), 1)
    ).astype(F32)
    counts = jnp.dot(earlier.astype(BF), onehot.astype(BF), preferred_element_type=F32)
    rank = jnp.sum(onehot * counts, axis=1, keepdims=True).astype(jnp.int32)
    step = dest.astype(jnp.int32) - 1 - own
    step = jnp.where(step < 0, step + experts, step)
    far = step - 1
    slot = jnp.where(rank < other, same + far * other, main + far * spare - other) + rank
    slot = jnp.where(rank < other + spare, slot, -1)
    slot = jnp.where(step > 0, slot, jnp.where(rank < same, rank, -1))
    slot = jnp.where(dest > 0.0, slot, -1)
    if ident is not None:
        slot = jnp.where(ident > 0, lax.broadcasted_iota(jnp.int32, slot.shape, 0), slot)
    lanes_out = lax.broadcasted_iota(jnp.int32, (rows, sum(sizes)), 1)
    return (lanes_out == slot).astype(F32).astype(BF)


def pack(places, rows, outs):
    packed = lax.dot_general(
        places, rows, (((0,), (0,)), ((), ())), preferred_element_type=F32
    )
    at = 0
    for out in outs:
        cap = out.shape[-2]
        out[...] = packed[at : at + cap].astype(BF).reshape(out.shape)
        at += cap


def whole(space=pltpu.VMEM):
    return pl.BlockSpec(memory_space=space)


def spans(width):
    units = width // 128
    pieces = 4 if units >= 8 else 1
    edges = [128 * (units * n // pieces) for n in range(pieces + 1)]
    return list(zip(edges[:-1], edges[1:]))


def load_call(w, rows, after):
    given, features = w.shape
    pieces = [(a, min(b, given)) for a, b in spans(rows)]

    def kernel(w_ref, _, out_ref, sems):
        copies = []
        for n, (start, stop) in enumerate(pieces):
            part = pl.ds(start, stop - start)
            copies.append(pltpu.make_async_copy(w_ref.at[part], out_ref.at[part], sems.at[n]))
            copies[n].start()
        if given < rows:
            out_ref[given:] = jnp.zeros((rows - given, features), out_ref.dtype)
        for copy in copies:
            copy.wait()

    return pl.pallas_call(
        kernel,
        in_specs=[whole(pl.ANY)] * 2,
        out_specs=whole(),
        out_shape=pltpu.VMEM((rows, features), w.dtype),
        scratch_shapes=[pltpu.SemaphoreType.DMA((len(pieces),))],
        compiler_params=pltpu.CompilerParams(vmem_limit_bytes=VMEM_LIMIT),
        cost_estimate=pl.CostEstimate(
            flops=0, bytes_accessed=4 * rows * features, transcendentals=0
        ),
        name="load",
    )(w, after)


def up_call(xs, gain, router_row, mask, w):
    count = len(xs)
    width, features = xs[0].shape[1], w.shape[1]
    rows = sum(x.shape[0] for x in xs)

    def kernel(*refs):
        gain_ref, router_ref, mask_ref, w_ref, out_ref = refs[count:]
        x = rows_of(refs[:count])
        kept = x * mask_ref[...]
        scaled = (x * gain_ref[...]).astype(BF)
        squares = jnp.sum(kept * kept, axis=1, keepdims=True)
        logits = jnp.sum(scaled.astype(F32) * router_ref[...], axis=1, keepdims=True)
        lanes = lax.broadcasted_iota(jnp.int32, (rows, 128), 1)
        stats = jnp.where(lanes == 0, squares, jnp.where(lanes == 1, logits, 0.0))
        out_ref[:, features:] = stats
        out_ref[:, :features] = jnp.dot(scaled, w_ref[...], preferred_element_type=F32)

    return pl.pallas_call(
        kernel,
        in_specs=[whole()] * (count + 3) + [whole()],
        out_specs=whole(),
        out_shape=jax.ShapeDtypeStruct((rows, features + 128), F32),
        compiler_params=pltpu.CompilerParams(vmem_limit_bytes=VMEM_LIMIT),
        cost_estimate=pl.CostEstimate(
            flops=2 * rows * width * features,
            bytes_accessed=2 * rows * width + 4 * rows * features,
            transcendentals=0,
        ),
        name="up",
    )(*xs, gain, router_row, mask, w)


def down_call(xs, partials, mask, w, scalars, injected, sizes, true_width, width_local):
    experts = lax.axis_size("expert")
    count, parts = len(xs), len(partials)
    width, features = xs[0].shape[1], w.shape[1]
    rows = sum(x.shape[0] for x in xs)
    pieces = spans(width)
    at = width_local - (width - 128)
    last = slice(width - 128, width)

    def kernel(*refs):
        refs = list(refs)
        scalar_ref = refs.pop(0)
        x_refs = [refs.pop(0) for _ in range(count)]
        part_refs = [refs.pop(0) for _ in range(parts)]
        mask_ref, w_ref = refs.pop(0), refs.pop(0)
        inj_refs = [refs.pop(0) for _ in injected]
        out_refs = refs

        total = part_refs[0][...]
        for other in part_refs[1:]:
            total = total + other[...]
        squares = total[:, features : features + 1]
        logits = total[:, features + 1 : features + 2]
        inv_rms = lax.rsqrt(squares / true_width + EPS)
        gate = jax.nn.sigmoid(logits * inv_rms)
        hidden = jax.nn.gelu(total[:, :features] * inv_rms).astype(BF)
        meta = jnp.concatenate([r[:, last].astype(F32) for r in x_refs], axis=0)
        ident = scalar_ref[2] if rows == sum(sizes) else None
        places = places_of(meta, at, scalar_ref[1], scalar_ref[3], sizes, experts, ident)
        if inj_refs:
            theirs = jnp.concatenate([r[:, last].astype(F32) for r in inj_refs], axis=0)
            which = lax.broadcasted_iota(jnp.int32, (8, 128), 0)
            lane = lax.broadcasted_iota(jnp.int32, (8, 128), 1)
            picks = ((lane == at + HOME + which) & (which < 3)).astype(F32).astype(BF)
            keys = lax.dot_general(
                picks, theirs.astype(BF), (((1,), (1,)), ((), ())), preferred_element_type=F32
            )
            home, low, high = (column(meta, at + HOME + n) for n in range(3))
            same = (home == keys[0:1]) & (low == keys[1:2]) & (high == keys[2:3])
            same = same & (home > 0.0) & (scalar_ref[4] > 0)
            match = same.astype(F32).astype(BF)

        for start, stop in pieces:
            cols = slice(start, stop)
            x = jnp.concatenate([r[:, cols].astype(F32) for r in x_refs], axis=0)
            out = lax.dot_general(
                hidden, w_ref[cols, :], (((1,), (1,)), ((), ())), preferred_element_type=F32
            ).astype(BF)
            updated = (x + gate * out.astype(F32)).astype(BF)
            state = jnp.where(scalar_ref[0] > 0, updated.astype(F32), x)
            if inj_refs:
                theirs = jnp.concatenate([r[:, cols].astype(F32) for r in inj_refs], axis=0)
                added = jnp.dot(match, theirs.astype(BF), preferred_element_type=F32)
                state = state + added * mask_ref[:, cols]
            packed = lax.dot_general(
                places, state.astype(BF), (((0,), (0,)), ((), ())), preferred_element_type=F32
            )
            row = 0
            for out_ref, n in zip(out_refs, sizes):
                out_ref[:, cols] = packed[row : row + n].astype(BF)
                row += n

    return pl.pallas_call(
        kernel,
        in_specs=[whole(pltpu.SMEM)]
        + [whole()] * (count + parts + 1)
        + [whole()]
        + [whole()] * len(injected),
        out_specs=[whole()] * len(sizes),
        out_shape=[jax.ShapeDtypeStruct((n, width), BF) for n in sizes],
        compiler_params=pltpu.CompilerParams(vmem_limit_bytes=VMEM_LIMIT),
        cost_estimate=pl.CostEstimate(
            flops=2 * rows * width * (features + sum(sizes)),
            bytes_accessed=4 * rows * width + 8 * rows * features,
            transcendentals=rows * features,
        ),
        name="down",
    )(scalars, *xs, *partials, mask, w, *injected)


def pack_call(rows_in, scalars, out_cap, experts, chunk, width_local):
    batches, rows, width = rows_in.shape
    at = width_local - (width - 128)
    last = width // 128 - 1

    def kernel(scalar_ref, x_ref, meta_ref, *refs):
        out_refs, places_ref = refs[:experts], refs[experts]

        @pl.when(pl.program_id(1) == 0)
        def _():
            meta = meta_ref[0].astype(F32)
            places_ref[...] = places_of(
                meta, at, scalar_ref[1], scalar_ref[3], [out_cap] * experts, experts, None
            )

        pack(places_ref[...], x_ref[0], out_refs)

    return pl.pallas_call(
        kernel,
        grid_spec=pltpu.PrefetchScalarGridSpec(
            num_scalar_prefetch=1,
            grid=(batches, width // chunk),
            in_specs=[
                pl.BlockSpec((1, rows, chunk), lambda j, c, s: (j, 0, c)),
                pl.BlockSpec((1, rows, 128), lambda j, c, s: (j, 0, last)),
            ],
            out_specs=[pl.BlockSpec((1, out_cap, chunk), lambda j, c, s: (j, 0, c))] * experts,
            scratch_shapes=[pltpu.VMEM((rows, experts * out_cap), BF)],
        ),
        out_shape=[jax.ShapeDtypeStruct((batches, out_cap, width), BF)] * experts,
        compiler_params=pltpu.CompilerParams(vmem_limit_bytes=VMEM_LIMIT),
        cost_estimate=pl.CostEstimate(
            flops=2 * batches * rows * width * experts * out_cap,
            bytes_accessed=4 * batches * rows * width,
            transcendentals=0,
        ),
        name="pack",
    )(scalars, rows_in, rows_in)


def unpack_call(groups, which, home_rows, chunk, width_local):
    width = groups[0][0].shape[1]
    at = width_local - (width - 128)
    last = width // 128 - 1
    flat = [b for g in groups for b in g]
    sizes = [len(g) for g in groups]
    totals = [sum(b.shape[0] for b in g) for g in groups]

    def kernel(scalar_ref, *refs):
        refs = list(refs)
        data = [[refs.pop(0) for _ in range(n)] for n in sizes]
        metas = [[refs.pop(0) for _ in range(n)] for n in sizes]
        out_ref = refs.pop(0)

        @pl.when(pl.program_id(0) == 0)
        def _():
            for g, ref in enumerate(refs):
                meta = rows_of(metas[g])
                low, high = column(meta, at + HOME + 1), column(meta, at + HOME + 2)
                token = (high * 128.0 + low).astype(jnp.int32) - 1
                lanes = lax.broadcasted_iota(jnp.int32, ref.shape, 1)
                hit = (lanes == token) & (scalar_ref[0] == g)
                ref[...] = hit.astype(F32).astype(BF)

        total = jnp.zeros(out_ref.shape, F32)
        for g, ref in enumerate(refs):
            total += lax.dot_general(
                ref[...],
                rows_of(data[g]).astype(BF),
                (((0,), (0,)), ((), ())),
                preferred_element_type=F32,
            )
        out_ref[...] = total.astype(BF)

    return pl.pallas_call(
        kernel,
        grid_spec=pltpu.PrefetchScalarGridSpec(
            num_scalar_prefetch=1,
            grid=(width // chunk,),
            in_specs=[pl.BlockSpec((b.shape[0], chunk), lambda c, s: (0, c)) for b in flat]
            + [pl.BlockSpec((b.shape[0], 128), lambda c, s: (0, last)) for b in flat],
            out_specs=pl.BlockSpec((home_rows, chunk), lambda c, s: (0, c)),
            scratch_shapes=[pltpu.VMEM((t, home_rows), BF) for t in totals],
        ),
        out_shape=jax.ShapeDtypeStruct((home_rows, width), BF),
        compiler_params=pltpu.CompilerParams(vmem_limit_bytes=VMEM_LIMIT),
        cost_estimate=pl.CostEstimate(
            flops=2 * sum(totals) * home_rows * width,
            bytes_accessed=2 * sum(totals) * width,
            transcendentals=0,
        ),
        name="unpack",
    )(which, *flat, *flat)


def dp_spread(rows, parts):
    lead, tokens, width = rows.shape
    w = width // parts
    me = lax.axis_index("dp")
    if parts == 2:
        low, high = rows[..., :w], rows[..., w:]
        mine = jnp.where(me == 0, low, high)
        theirs = lax.ppermute(jnp.where(me == 0, high, low), "dp", [(0, 1), (1, 0)])
        first = jnp.where(me == 0, mine, theirs)
        second = jnp.where(me == 0, theirs, mine)
        return jnp.concatenate([first, second], axis=1)
    split = rows.reshape(lead, tokens, parts, w).transpose(2, 0, 1, 3)
    got = lax.all_to_all(split, "dp", 0, 0, tiled=True)
    return got.transpose(1, 0, 2, 3).reshape(lead, parts * tokens, w)


def dp_return(rows, parts):
    tokens, w = rows.shape[0] // parts, rows.shape[1]
    me = lax.axis_index("dp")
    if parts == 2:
        low, high = rows[:tokens], rows[tokens:]
        mine = jnp.where(me == 0, low, high)
        theirs = lax.ppermute(jnp.where(me == 0, high, low), "dp", [(0, 1), (1, 0)])
        return jnp.where(
            me == 0,
            jnp.concatenate([mine, theirs], axis=1),
            jnp.concatenate([theirs, mine], axis=1),
        )
    got = lax.all_to_all(rows.reshape(parts, tokens, w), "dp", 0, 0, tiled=True)
    return got.transpose(1, 0, 2).reshape(tokens, parts * w)


def dp_partials(partial, parts):
    if parts == 2:
        return [partial, lax.ppermute(partial, "dp", [(0, 1), (1, 0)])]
    return [lax.psum(partial, "dp")]


def gathered_routes(routes, sections, parts):
    own = routes[:, 0, :, :, 0]
    me = lax.axis_index("section")
    blocks = lax.broadcasted_iota(jnp.int32, (1, sections, 1, 1), 1)
    every = jnp.zeros(own.shape[:1] + (sections,) + own.shape[1:], jnp.int32)
    for k in range(sections):
        got = own if k == 0 else shifted(own, "section", k)
        every = jnp.where(blocks == jnp.mod(me - k, sections), got[:, None], every)
    every = every.reshape((-1,) + own.shape[1:])
    if parts == 2:
        other = lax.ppermute(every, "dp", [(0, 1), (1, 0)])
        first = lax.axis_index("dp") == 0
        return jnp.concatenate(
            [jnp.where(first, every, other), jnp.where(first, other, every)], axis=-1
        )
    return lax.all_gather(every, "dp", axis=2, tiled=True)


def pair_counts(routes, experts):
    labels = jnp.arange(experts, dtype=jnp.int32)
    onehot = (routes[..., None] == labels).astype(BF)
    counts = jnp.einsum(
        "imta,imtb->imab", onehot[:-1], onehot[1:], preferred_element_type=F32
    )
    total = counts
    for k in range(1, experts):
        total = total + shifted(counts, "expert", k)
    like = (labels[:, None] == labels[None, :])[None, None]
    other = jnp.max(jnp.where(like, 0.0, total), axis=(2, 3))
    same = jnp.max(jnp.where(like, total, 0.0), axis=(2, 3))
    return other, same


def joint_pairs(moves, experts, k):
    return [
        (a * experts + e, b * experts + (e + k) % experts) for a, b in moves for e in range(experts)
    ]


def move(bufs, moves, experts, straight=()):
    kept = joint_pairs(straight, experts, 0)
    return [
        lax.ppermute(buf, JOINT, joint_pairs(moves, experts, k) + kept)
        for k, buf in enumerate(bufs)
    ]


def move_spare(bufs, needed, moves, experts, w, width, straight=()):
    kept = joint_pairs(straight, experts, 0)
    bufs = list(bufs)

    def send(spare):
        n = spare.shape[0] // (experts - 1)
        return jnp.concatenate(
            [
                lax.ppermute(
                    spare[k * n : (k + 1) * n], JOINT, joint_pairs(moves, experts, k + 1) + kept
                )
                for k in range(experts - 1)
            ]
        )

    main = move(bufs[:experts], moves, experts, straight)
    held = load_call(w, width, bufs[0])
    if needed is None:
        spare = send(bufs[experts])
    else:
        spare = lax.cond(needed, send, lambda spare: spare, bufs[experts])
    return main + [spare], held


def move_within(bufs, section, experts):
    return [bufs[0]] + [
        lax.ppermute(bufs[k], JOINT, joint_pairs([(section, section)], experts, k))
        for k in range(1, experts)
    ]


def direct_body(init_state, inject, routes, norm_gain, router, w_up, w_down):
    sections, parts, experts = (lax.axis_size(a) for a in ("section", "dp", "expert"))
    section, own = lax.axis_index("section"), lax.axis_index("expert")
    micro, tokens, true_width = init_state.shape
    w = true_width // parts
    width = -(-(w + META) // 128) * 128
    chunk = width
    home = parts * tokens
    home_cap = CAP * parts
    same_cap, other_cap, spare_cap = SAME_CAP * parts, OTHER_CAP * parts, SPARE_CAP * parts
    sizes = [same_cap] + [other_cap] * (experts - 1) + [spare_cap * (experts - 1)]
    order = [(sections - 2 - j) % sections for j in range(micro)]
    pad = width - w

    all_routes = gathered_routes(routes, sections, parts)
    position = np.argsort(np.array(order))
    moment = np.arange(all_routes.shape[0] - 1)[:, None] + position[None, :]
    when = np.arange(sections * RECUR + sections - 2)[:, None, None] == moment[None]

    mask = (lax.broadcasted_iota(jnp.int32, (1, width), 1) < w).astype(F32)
    gain = lax.dynamic_slice(norm_gain, (0, lax.axis_index("dp") * w), (1, w))
    gain = jnp.pad(gain, ((0, 0), (0, pad)))
    router_row = lax.dynamic_slice(router, (0, own, lax.axis_index("dp") * w), (1, 1, w))[0]
    router_row = jnp.pad(router_row.astype(F32), ((0, 0), (0, pad)))
    w_first, w_second = w_up[0, 0], w_down[0, 0].T
    if w % 16:
        short = ((0, pad), (0, 0))
        w_first, w_second = jnp.pad(w_first, short), jnp.pad(w_second, short)

    token = lax.broadcasted_iota(jnp.int32, (1, micro, home), 2)
    homes = jnp.broadcast_to(own + 1, token.shape).astype(jnp.int32)
    fields = jnp.concatenate([all_routes + 1, homes, token % 128 + 1, token // 128], axis=0)
    fields = jnp.transpose(fields, (1, 2, 0)).astype(BF)
    fields = jnp.pad(fields, ((0, 0), (0, 0), (0, pad - fields.shape[-1])))

    def with_fields(spread, picked):
        return jnp.concatenate([spread, picked], axis=-1)

    def entry(m):
        return (init_state[m].astype(F32) + inject[m].astype(F32)).astype(BF)

    first = entry(order[0])[None]
    rest = jnp.stack([entry(m) for m in order[1:]])
    injected = jnp.stack([inject[m] for m in order])
    live_fields = jnp.stack([fields[m] for m in order])
    last_section = section == sections - 1
    injected_rows = with_fields(dp_spread(injected, parts), live_fields)
    entry_rows = with_fields(
        dp_spread(jnp.concatenate([first, rest]), parts), live_fields
    )
    nothing = jnp.zeros((), BF)
    opening = jnp.where(last_section, injected_rows[:1], entry_rows[:1])
    opening = jnp.where((section == 0) | last_section, opening, nothing)

    def scalars(live, next_idx, ident, add):
        values = [live, next_idx, ident, own, add]
        return jnp.stack([jnp.asarray(v, jnp.int32) for v in values])

    sent = pack_call(
        opening,
        scalars(0, jnp.where(last_section, sections - 1, 0), 0, 0),
        home_cap,
        experts,
        chunk,
        w,
    )
    sent = [b[0] for b in sent]
    bufs = [sent[0]] + [
        lax.ppermute(
            sent[k], JOINT, joint_pairs([(0, 0), (sections - 1, sections - 1)], experts, k)
        )
        for k in range(1, experts)
    ]

    first_held = load_call(w_first, width, sent[0])
    ring = [(s, (s + 1) % sections) for s in range(sections)]
    span = sections * RECUR
    total_steps = span + sections - 1
    finals = {}
    ahead = []
    for t in range(total_steps):
        if t < micro - 1:
            entering = jnp.where(last_section, entry_rows[t + 1], nothing)
            fill = last_section
            ahead.append(list(bufs))
            if t < sections - 2:
                entering = jnp.where(section == sections - 2, injected_rows[t + 1], entering)
                fill = fill | (section == sections - 2)
            at = 0
            for k, buf in enumerate(bufs):
                n = buf.shape[0]
                part = entering[at : at + n]
                part = jnp.pad(part, ((0, n - part.shape[0]), (0, 0)))
                bufs[k] = jnp.where(fill, part, buf)
                at += n
        if t == 1:
            bufs, late, crowded = lax.optimization_barrier((bufs, late, crowded))
        offset = t - section
        live = (offset >= 0) & (offset < span)
        round_of = jnp.clip(offset, 0, span - 1) // sections
        next_idx = jnp.where(live, round_of * sections + section + 1, 0)
        if t < sections - 2:
            next_idx = jnp.where(section == sections - 2, sections - 1, next_idx)
        partial = up_call(bufs, gain, router_row, mask, first_held)
        second_held = load_call(w_second, width, partial)
        partials = dp_partials(partial, parts)
        adding = sections - 1 <= t < 2 * sections - 1
        is_last = t == total_steps - 1
        ident = (section == 0) & (t >= span)
        outs = down_call(
            bufs,
            partials,
            mask,
            second_held,
            scalars(live, next_idx, ident, last_section & adding),
            (ahead + [late])[t - sections + 1] if adding else [],
            [home_cap] * experts if is_last else sizes,
            true_width,
            w,
        )
        if t == 0:
            outs, late_rows, all_routes = lax.optimization_barrier(
                (outs, injected_rows[micro - 1 :], all_routes)
            )
            other, same = pair_counts(all_routes, experts)
            overflow = (jnp.max(other) > other_cap + spare_cap) | (jnp.max(same) > same_cap)
            crowded = jnp.max(jnp.where(when, other[None], 0.0), axis=(1, 2)) > other_cap
            late = pack_call(
                late_rows, scalars(0, sections - 1, 0, 0), home_cap, experts, chunk, w
            )
            late = move([b[0] for b in late], [(1, sections - 1)], experts)
        if is_last:
            finals[sections - 1] = move_within(outs, sections - 1, experts)
        elif t < span:
            bufs, first_held = move_spare(
                outs, crowded[t] if t else None, ring, experts, w_first, width
            )
        else:
            j = t - (sections - 1) - sections
            target = order[j]
            moves = [(s, s + 1) for s in range(t - span + 1, sections - 1)]
            moves.append((sections - 1, target))
            passing = (0, 0) if t < total_steps - 2 else (0, order[0])
            bufs, first_held = move_spare(
                outs, crowded[t], moves, experts, w_first, width, [passing]
            )
            finals[target] = bufs[:experts]
            if t == total_steps - 2:
                finals[order[0]] = bufs[:experts]

    groups = [finals[1], finals[0], finals[sections - 1]]
    which = jnp.where(section == 1, 0, jnp.where(last_section, 2, 1)).astype(jnp.int32)
    rows = unpack_call(groups, which.reshape(1), home, chunk, w)
    result = dp_return(rows[:, :w], parts)
    return result[None], overflow


def body(*arguments):
    result, overflow = direct_body(*arguments)
    return lax.cond(overflow, lambda: general_body(*arguments), lambda: result)


def solution(mesh):
    return jax.shard_map(
        body,
        mesh=mesh,
        in_specs=(
            P(None, ("dp", "expert"), None),
            P(None, ("dp", "expert"), None),
            P(None, "section", None, ("dp", "expert"), None),
            P("section", None),
            P("section", None, None),
            P("section", "expert", "dp", None),
            P("section", "expert", None, "dp"),
        ),
        out_specs=P("section", ("dp", "expert"), None),
        check_vma=False,
    )
```

```python
import functools
import jax
import jax.numpy as jnp
import numpy as np
from jax import lax
from jax.experimental import pallas as pl
from jax.experimental.pallas import tpu as pltpu
from jax.sharding import PartitionSpec as P

RECUR = 2
CAP = 12
SAME_CAP = 20
OTHER_CAP = 16
SPARE_CAP = 4
META = 16
HOME = 8
EPS = 1e-05
VMEM_LIMIT = 16 << 20
BF = jnp.bfloat16
F32 = jnp.float32
JOINT = ("section", "expert")


def shifted(block, axis, distance):
    devices = range(lax.axis_size(axis))
    route = [((i - distance) % len(devices), i) for i in devices]
    return lax.ppermute(block, axis, route)


def normalize(current, gain_row):
    as_float = current.astype(F32)
    inv_rms = lax.rsqrt(jnp.mean(as_float * as_float, axis=-1, keepdims=True) + EPS)
    return (as_float * inv_rms * gain_row).astype(BF)


def expert_rows(item_rows, w_first, w_second):
    extent = item_rows.shape
    flat_rows = item_rows.reshape(-1, extent[-1])
    hidden = jax.nn.gelu(jnp.dot(flat_rows, w_first, preferred_element_type=F32)).astype(BF)
    result = jnp.dot(hidden, w_second, preferred_element_type=F32).astype(BF)
    return result.reshape(extent)


def whole_round(buffer, w_first, w_second):
    processed = expert_rows(
        lax.all_to_all(buffer, "expert", split_axis=0, concat_axis=0, tiled=True), w_first, w_second
    )
    return lax.all_to_all(processed, "expert", split_axis=0, concat_axis=0, tiled=True)


def core_block(current, gain_row, router_rows, w_first, w_second, assign):
    tokens = current.shape[0]
    experts = router_rows.shape[0]
    normed = normalize(current, gain_row)
    logits = jnp.dot(normed, router_rows.T, preferred_element_type=F32)
    labels = lax.broadcasted_iota(jnp.int32, (tokens, experts), 1)
    onehot = (assign[:, None] == labels).astype(F32)
    gate_value = jax.nn.sigmoid(jnp.sum(onehot * logits, axis=-1))
    earlier = (
        lax.broadcasted_iota(jnp.int32, (tokens, tokens), 0)
        > lax.broadcasted_iota(jnp.int32, (tokens, tokens), 1)
    ).astype(F32)
    counts = jnp.dot(earlier, onehot, preferred_element_type=F32)
    slot_index = jnp.sum(onehot * counts, axis=-1).astype(jnp.int32)
    target = assign * CAP + slot_index
    places = (
        lax.broadcasted_iota(jnp.int32, (experts * CAP, tokens), 0) == target[None, :]
    ).astype(BF)
    buffer = (
        jnp.dot(places, normed, preferred_element_type=F32).astype(BF).reshape(experts, CAP, -1)
    )
    returned = whole_round(buffer, w_first, w_second)
    flat_back = returned.reshape(experts * CAP, -1)
    expert_out = jnp.einsum("st,sd->td", places, flat_back, preferred_element_type=F32)
    updated = current.astype(F32) + gate_value[:, None] * expert_out
    return updated.astype(BF)


def general_body(init_state, inject, routes, norm_gain, router, w_up, w_down):
    sections = lax.axis_size("section")
    section_index = lax.axis_index("section")
    w_first = lax.all_gather(w_up, "dp", axis=2, tiled=True)[0, 0]
    w_second = lax.all_gather(w_down, "dp", axis=3, tiled=True)[0, 0]
    gain_row = norm_gain[0]
    router_rows = router[0]
    tokens = init_state.shape[1]
    active_span = sections * RECUR
    total_steps = active_span + sections - 1

    def advance(moment, hidden_state):
        offset = moment - section_index
        is_live = (offset >= 0) & (offset < active_span)
        clipped = jnp.clip(offset, 0, active_span - 1)
        loop_round = clipped // sections
        entry_slot = clipped % sections
        micro_idx = jnp.mod(sections - 2 - entry_slot, sections)
        initial = lax.dynamic_index_in_dim(init_state, micro_idx, 0, keepdims=False)
        injected_row = lax.dynamic_index_in_dim(inject, micro_idx, 0, keepdims=False)
        incoming = jnp.where(loop_round == 0, initial, hidden_state)
        injected = (incoming.astype(F32) + injected_row.astype(F32)).astype(BF)
        entering = is_live & (section_index == 0)
        current = jnp.where(entering, injected, hidden_state)
        assign = lax.dynamic_slice(
            routes, (loop_round, 0, micro_idx, 0, 0), (1, 1, 1, tokens, 1)
        ).reshape(tokens)
        result = core_block(current, gain_row, router_rows, w_first, w_second, assign)
        return jnp.where(is_live, result, hidden_state)

    def advance_one(moment, hidden_state):
        return advance(moment, shifted(hidden_state, "section", 1))

    hidden_state = jnp.zeros(init_state.shape[1:], BF)
    hidden_state = advance(0, hidden_state)
    hidden_state = lax.fori_loop(1, total_steps, advance_one, hidden_state)
    return hidden_state[None]


def rows_of(refs):
    return jnp.concatenate([r[...].astype(F32) for r in refs], axis=0)


def column(block, index):
    lanes = lax.broadcasted_iota(jnp.int32, block.shape, 1)
    return jnp.sum(jnp.where(lanes == index, block, 0.0), axis=1, keepdims=True)


def places_of(meta, at, next_idx, own, sizes, experts, ident):
    same, other = sizes[0], sizes[1]
    spare = sizes[experts] // (experts - 1) if len(sizes) > experts else 0
    main = same + (experts - 1) * other
    rows = meta.shape[0]
    dest = column(meta, at + next_idx)
    lanes = lax.broadcasted_iota(jnp.int32, meta.shape, 1)
    onehot = (((lanes + 1).astype(F32) == dest) & (lanes < experts)).astype(F32)
    earlier = (
        lax.broadcasted_iota(jnp.int32, (rows, rows), 0)
        > lax.broadcasted_iota(jnp.int32, (rows, rows), 1)
    ).astype(F32)
    counts = jnp.dot(earlier.astype(BF), onehot.astype(BF), preferred_element_type=F32)
    rank = jnp.sum(onehot * counts, axis=1, keepdims=True).astype(jnp.int32)
    step = dest.astype(jnp.int32) - 1 - own
    step = jnp.where(step < 0, step + experts, step)
    far = step - 1
    slot = jnp.where(rank < other, same + far * other, main + far * spare - other) + rank
    slot = jnp.where(rank < other + spare, slot, -1)
    slot = jnp.where(step > 0, slot, jnp.where(rank < same, rank, -1))
    slot = jnp.where(dest > 0.0, slot, -1)
    if ident is not None:
        slot = jnp.where(ident > 0, lax.broadcasted_iota(jnp.int32, slot.shape, 0), slot)
    lanes_out = lax.broadcasted_iota(jnp.int32, (rows, sum(sizes)), 1)
    return (lanes_out == slot).astype(F32).astype(BF)


def pack(places, rows, outs):
    packed = lax.dot_general(
        places, rows, (((0,), (0,)), ((), ())), preferred_element_type=F32
    )
    at = 0
    for out in outs:
        cap = out.shape[-2]
        out[...] = packed[at : at + cap].astype(BF).reshape(out.shape)
        at += cap


def whole(space=pltpu.VMEM):
    return pl.BlockSpec(memory_space=space)


def spans(width):
    units = width // 128
    pieces = 2 if units >= 8 else 1
    edges = [128 * (units * n // pieces) for n in range(pieces + 1)]
    return list(zip(edges[:-1], edges[1:]))


def load_call(w, rows, after):
    given, features = w.shape

    def kernel(w_ref, _, out_ref, sem):
        copy = pltpu.make_async_copy(w_ref, out_ref.at[pl.ds(0, given)], sem)
        copy.start()
        if given < rows:
            out_ref[given:] = jnp.zeros((rows - given, features), out_ref.dtype)
        copy.wait()

    return pl.pallas_call(
        kernel,
        in_specs=[whole(pl.ANY)] * 2,
        out_specs=whole(),
        out_shape=pltpu.VMEM((rows, features), w.dtype),
        scratch_shapes=[pltpu.SemaphoreType.DMA],
        compiler_params=pltpu.CompilerParams(vmem_limit_bytes=VMEM_LIMIT),
        cost_estimate=pl.CostEstimate(
            flops=0, bytes_accessed=4 * rows * features, transcendentals=0
        ),
        name="load",
    )(w, after)


def up_call(xs, gain, router_row, mask, w):
    count = len(xs)
    width, features = xs[0].shape[1], w.shape[1]
    rows = sum(x.shape[0] for x in xs)

    def kernel(*refs):
        gain_ref, router_ref, mask_ref, w_ref, out_ref = refs[count:]
        x = rows_of(refs[:count])
        kept = x * mask_ref[...]
        scaled = (x * gain_ref[...]).astype(BF)
        squares = jnp.sum(kept * kept, axis=1, keepdims=True)
        logits = jnp.sum(scaled.astype(F32) * router_ref[...], axis=1, keepdims=True)
        lanes = lax.broadcasted_iota(jnp.int32, (rows, 128), 1)
        stats = jnp.where(lanes == 0, squares, jnp.where(lanes == 1, logits, 0.0))
        out_ref[:, features:] = stats
        out_ref[:, :features] = jnp.dot(scaled, w_ref[...], preferred_element_type=F32)

    return pl.pallas_call(
        kernel,
        in_specs=[whole()] * (count + 3) + [whole()],
        out_specs=whole(),
        out_shape=jax.ShapeDtypeStruct((rows, features + 128), F32),
        compiler_params=pltpu.CompilerParams(vmem_limit_bytes=VMEM_LIMIT),
        cost_estimate=pl.CostEstimate(
            flops=2 * rows * width * features,
            bytes_accessed=2 * rows * width + 4 * rows * features,
            transcendentals=0,
        ),
        name="up",
    )(*xs, gain, router_row, mask, w)


def down_call(xs, partials, mask, w, scalars, injected, sizes, true_width, width_local):
    experts = lax.axis_size("expert")
    count, parts = len(xs), len(partials)
    width, features = xs[0].shape[1], w.shape[1]
    rows = sum(x.shape[0] for x in xs)
    pieces = spans(width)
    at = width_local - (width - 128)
    last = slice(width - 128, width)

    def kernel(*refs):
        refs = list(refs)
        scalar_ref = refs.pop(0)
        x_refs = [refs.pop(0) for _ in range(count)]
        part_refs = [refs.pop(0) for _ in range(parts)]
        mask_ref, w_ref = refs.pop(0), refs.pop(0)
        inj_refs = [refs.pop(0) for _ in injected]
        out_refs = refs

        total = part_refs[0][...]
        for other in part_refs[1:]:
            total = total + other[...]
        squares = total[:, features : features + 1]
        logits = total[:, features + 1 : features + 2]
        inv_rms = lax.rsqrt(squares / true_width + EPS)
        gate = jax.nn.sigmoid(logits * inv_rms)
        hidden = jax.nn.gelu(total[:, :features] * inv_rms).astype(BF)
        meta = jnp.concatenate([r[:, last].astype(F32) for r in x_refs], axis=0)
        ident = scalar_ref[2] if rows == sum(sizes) else None
        places = places_of(meta, at, scalar_ref[1], scalar_ref[3], sizes, experts, ident)
        if inj_refs:
            theirs = jnp.concatenate([r[:, last].astype(F32) for r in inj_refs], axis=0)
            which = lax.broadcasted_iota(jnp.int32, (8, 128), 0)
            lane = lax.broadcasted_iota(jnp.int32, (8, 128), 1)
            picks = ((lane == at + HOME + which) & (which < 3)).astype(F32).astype(BF)
            keys = lax.dot_general(
                picks, theirs.astype(BF), (((1,), (1,)), ((), ())), preferred_element_type=F32
            )
            home, low, high = (column(meta, at + HOME + n) for n in range(3))
            same = (home == keys[0:1]) & (low == keys[1:2]) & (high == keys[2:3])
            same = same & (home > 0.0) & (scalar_ref[4] > 0)
            match = same.astype(F32).astype(BF)

        for start, stop in pieces:
            cols = slice(start, stop)
            x = jnp.concatenate([r[:, cols].astype(F32) for r in x_refs], axis=0)
            out = lax.dot_general(
                hidden, w_ref[cols, :], (((1,), (1,)), ((), ())), preferred_element_type=F32
            ).astype(BF)
            updated = (x + gate * out.astype(F32)).astype(BF)
            state = jnp.where(scalar_ref[0] > 0, updated.astype(F32), x)
            if inj_refs:
                theirs = jnp.concatenate([r[:, cols].astype(F32) for r in inj_refs], axis=0)
                added = jnp.dot(match, theirs.astype(BF), preferred_element_type=F32)
                state = state + added * mask_ref[:, cols]
            packed = lax.dot_general(
                places, state.astype(BF), (((0,), (0,)), ((), ())), preferred_element_type=F32
            )
            row = 0
            for out_ref, n in zip(out_refs, sizes):
                out_ref[:, cols] = packed[row : row + n].astype(BF)
                row += n

    return pl.pallas_call(
        kernel,
        in_specs=[whole(pltpu.SMEM)]
        + [whole()] * (count + parts + 1)
        + [whole()]
        + [whole()] * len(injected),
        out_specs=[whole()] * len(sizes),
        out_shape=[jax.ShapeDtypeStruct((n, width), BF) for n in sizes],
        compiler_params=pltpu.CompilerParams(vmem_limit_bytes=VMEM_LIMIT),
        cost_estimate=pl.CostEstimate(
            flops=2 * rows * width * (features + sum(sizes)),
            bytes_accessed=4 * rows * width + 8 * rows * features,
            transcendentals=rows * features,
        ),
        name="down",
    )(scalars, *xs, *partials, mask, w, *injected)


def pack_call(rows_in, scalars, out_cap, experts, chunk, width_local):
    batches, rows, width = rows_in.shape
    at = width_local - (width - 128)
    last = width // 128 - 1

    def kernel(scalar_ref, x_ref, meta_ref, *refs):
        out_refs, places_ref = refs[:experts], refs[experts]

        @pl.when(pl.program_id(1) == 0)
        def _():
            meta = meta_ref[0].astype(F32)
            places_ref[...] = places_of(
                meta, at, scalar_ref[1], scalar_ref[3], [out_cap] * experts, experts, None
            )

        pack(places_ref[...], x_ref[0], out_refs)

    return pl.pallas_call(
        kernel,
        grid_spec=pltpu.PrefetchScalarGridSpec(
            num_scalar_prefetch=1,
            grid=(batches, width // chunk),
            in_specs=[
                pl.BlockSpec((1, rows, chunk), lambda j, c, s: (j, 0, c)),
                pl.BlockSpec((1, rows, 128), lambda j, c, s: (j, 0, last)),
            ],
            out_specs=[pl.BlockSpec((1, out_cap, chunk), lambda j, c, s: (j, 0, c))] * experts,
            scratch_shapes=[pltpu.VMEM((rows, experts * out_cap), BF)],
        ),
        out_shape=[jax.ShapeDtypeStruct((batches, out_cap, width), BF)] * experts,
        compiler_params=pltpu.CompilerParams(vmem_limit_bytes=VMEM_LIMIT),
        cost_estimate=pl.CostEstimate(
            flops=2 * batches * rows * width * experts * out_cap,
            bytes_accessed=4 * batches * rows * width,
            transcendentals=0,
        ),
        name="pack",
    )(scalars, rows_in, rows_in)


def unpack_call(groups, which, home_rows, chunk, width_local):
    width = groups[0][0].shape[1]
    at = width_local - (width - 128)
    last = width // 128 - 1
    flat = [b for g in groups for b in g]
    sizes = [len(g) for g in groups]
    totals = [sum(b.shape[0] for b in g) for g in groups]

    def kernel(scalar_ref, *refs):
        refs = list(refs)
        data = [[refs.pop(0) for _ in range(n)] for n in sizes]
        metas = [[refs.pop(0) for _ in range(n)] for n in sizes]
        out_ref = refs.pop(0)

        @pl.when(pl.program_id(0) == 0)
        def _():
            for g, ref in enumerate(refs):
                meta = rows_of(metas[g])
                low, high = column(meta, at + HOME + 1), column(meta, at + HOME + 2)
                token = (high * 128.0 + low).astype(jnp.int32) - 1
                lanes = lax.broadcasted_iota(jnp.int32, ref.shape, 1)
                hit = (lanes == token) & (scalar_ref[0] == g)
                ref[...] = hit.astype(F32).astype(BF)

        total = jnp.zeros(out_ref.shape, F32)
        for g, ref in enumerate(refs):
            total += lax.dot_general(
                ref[...],
                rows_of(data[g]).astype(BF),
                (((0,), (0,)), ((), ())),
                preferred_element_type=F32,
            )
        out_ref[...] = total.astype(BF)

    return pl.pallas_call(
        kernel,
        grid_spec=pltpu.PrefetchScalarGridSpec(
            num_scalar_prefetch=1,
            grid=(width // chunk,),
            in_specs=[pl.BlockSpec((b.shape[0], chunk), lambda c, s: (0, c)) for b in flat]
            + [pl.BlockSpec((b.shape[0], 128), lambda c, s: (0, last)) for b in flat],
            out_specs=pl.BlockSpec((home_rows, chunk), lambda c, s: (0, c)),
            scratch_shapes=[pltpu.VMEM((t, home_rows), BF) for t in totals],
        ),
        out_shape=jax.ShapeDtypeStruct((home_rows, width), BF),
        compiler_params=pltpu.CompilerParams(vmem_limit_bytes=VMEM_LIMIT),
        cost_estimate=pl.CostEstimate(
            flops=2 * sum(totals) * home_rows * width,
            bytes_accessed=2 * sum(totals) * width,
            transcendentals=0,
        ),
        name="unpack",
    )(which, *flat, *flat)


def dp_spread(rows, parts):
    lead, tokens, width = rows.shape
    w = width // parts
    me = lax.axis_index("dp")
    if parts == 2:
        low, high = rows[..., :w], rows[..., w:]
        mine = jnp.where(me == 0, low, high)
        theirs = lax.ppermute(jnp.where(me == 0, high, low), "dp", [(0, 1), (1, 0)])
        first = jnp.where(me == 0, mine, theirs)
        second = jnp.where(me == 0, theirs, mine)
        return jnp.concatenate([first, second], axis=1)
    split = rows.reshape(lead, tokens, parts, w).transpose(2, 0, 1, 3)
    got = lax.all_to_all(split, "dp", 0, 0, tiled=True)
    return got.transpose(1, 0, 2, 3).reshape(lead, parts * tokens, w)


def dp_return(rows, parts):
    tokens, w = rows.shape[0] // parts, rows.shape[1]
    me = lax.axis_index("dp")
    if parts == 2:
        low, high = rows[:tokens], rows[tokens:]
        mine = jnp.where(me == 0, low, high)
        theirs = lax.ppermute(jnp.where(me == 0, high, low), "dp", [(0, 1), (1, 0)])
        return jnp.where(
            me == 0,
            jnp.concatenate([mine, theirs], axis=1),
            jnp.concatenate([theirs, mine], axis=1),
        )
    got = lax.all_to_all(rows.reshape(parts, tokens, w), "dp", 0, 0, tiled=True)
    return got.transpose(1, 0, 2).reshape(tokens, parts * w)


def dp_partials(partial, parts):
    if parts == 2:
        return [partial, lax.ppermute(partial, "dp", [(0, 1), (1, 0)])]
    return [lax.psum(partial, "dp")]


def gathered_routes(routes, sections, parts):
    own = routes[:, 0, :, :, 0]
    me = lax.axis_index("section")
    blocks = lax.broadcasted_iota(jnp.int32, (1, sections, 1, 1), 1)
    every = jnp.zeros(own.shape[:1] + (sections,) + own.shape[1:], jnp.int32)
    for k in range(sections):
        got = own if k == 0 else shifted(own, "section", k)
        every = jnp.where(blocks == jnp.mod(me - k, sections), got[:, None], every)
    every = every.reshape((-1,) + own.shape[1:])
    if parts == 2:
        other = lax.ppermute(every, "dp", [(0, 1), (1, 0)])
        first = lax.axis_index("dp") == 0
        return jnp.concatenate(
            [jnp.where(first, every, other), jnp.where(first, other, every)], axis=-1
        )
    return lax.all_gather(every, "dp", axis=2, tiled=True)


def pair_counts(routes, experts):
    labels = jnp.arange(experts, dtype=jnp.int32)
    onehot = (routes[..., None] == labels).astype(BF)
    counts = jnp.einsum(
        "imta,imtb->imab", onehot[:-1], onehot[1:], preferred_element_type=F32
    )
    total = counts
    for k in range(1, experts):
        total = total + shifted(counts, "expert", k)
    like = (labels[:, None] == labels[None, :])[None, None]
    other = jnp.max(jnp.where(like, 0.0, total), axis=(2, 3))
    same = jnp.max(jnp.where(like, total, 0.0), axis=(2, 3))
    return other, same


def joint_pairs(moves, experts, k):
    return [
        (a * experts + e, b * experts + (e + k) % experts) for a, b in moves for e in range(experts)
    ]


def move(bufs, moves, experts, straight=()):
    kept = joint_pairs(straight, experts, 0)
    return [
        lax.ppermute(buf, JOINT, joint_pairs(moves, experts, k) + kept)
        for k, buf in enumerate(bufs)
    ]


def move_spare(bufs, needed, moves, experts, w, width, straight=()):
    kept = joint_pairs(straight, experts, 0)
    bufs = list(bufs)

    def send(spare):
        n = spare.shape[0] // (experts - 1)
        return jnp.concatenate(
            [
                lax.ppermute(
                    spare[k * n : (k + 1) * n], JOINT, joint_pairs(moves, experts, k + 1) + kept
                )
                for k in range(experts - 1)
            ]
        )

    main = move(bufs[:experts], moves, experts, straight)
    held = load_call(w, width, bufs[0])
    if needed is None:
        spare = send(bufs[experts])
    else:
        spare = lax.cond(needed, send, lambda spare: spare, bufs[experts])
    return main + [spare], held


def move_within(bufs, section, experts):
    return [bufs[0]] + [
        lax.ppermute(bufs[k], JOINT, joint_pairs([(section, section)], experts, k))
        for k in range(1, experts)
    ]


def direct_body(init_state, inject, routes, norm_gain, router, w_up, w_down):
    sections, parts, experts = (lax.axis_size(a) for a in ("section", "dp", "expert"))
    section, own = lax.axis_index("section"), lax.axis_index("expert")
    micro, tokens, true_width = init_state.shape
    w = true_width // parts
    width = -(-(w + META) // 128) * 128
    chunk = width
    home = parts * tokens
    home_cap = CAP * parts
    same_cap, other_cap, spare_cap = SAME_CAP * parts, OTHER_CAP * parts, SPARE_CAP * parts
    sizes = [same_cap] + [other_cap] * (experts - 1) + [spare_cap * (experts - 1)]
    order = [(sections - 2 - j) % sections for j in range(micro)]
    pad = width - w

    all_routes = gathered_routes(routes, sections, parts)
    position = np.argsort(np.array(order))
    moment = np.arange(all_routes.shape[0] - 1)[:, None] + position[None, :]
    when = np.arange(sections * RECUR + sections - 2)[:, None, None] == moment[None]

    mask = (lax.broadcasted_iota(jnp.int32, (1, width), 1) < w).astype(F32)
    gain = lax.dynamic_slice(norm_gain, (0, lax.axis_index("dp") * w), (1, w))
    gain = jnp.pad(gain, ((0, 0), (0, pad)))
    router_row = lax.dynamic_slice(router, (0, own, lax.axis_index("dp") * w), (1, 1, w))[0]
    router_row = jnp.pad(router_row.astype(F32), ((0, 0), (0, pad)))
    w_first, w_second = w_up[0, 0], w_down[0, 0].T
    if w % 16:
        short = ((0, pad), (0, 0))
        w_first, w_second = jnp.pad(w_first, short), jnp.pad(w_second, short)

    token = lax.broadcasted_iota(jnp.int32, (1, micro, home), 2)
    homes = jnp.broadcast_to(own + 1, token.shape).astype(jnp.int32)
    fields = jnp.concatenate([all_routes + 1, homes, token % 128 + 1, token // 128], axis=0)
    fields = jnp.transpose(fields, (1, 2, 0)).astype(BF)
    fields = jnp.pad(fields, ((0, 0), (0, 0), (0, pad - fields.shape[-1])))

    def with_fields(spread, picked):
        return jnp.concatenate([spread, picked], axis=-1)

    def entry(m):
        return (init_state[m].astype(F32) + inject[m].astype(F32)).astype(BF)

    first = entry(order[0])[None]
    rest = jnp.stack([entry(m) for m in order[1:]])
    injected = jnp.stack([inject[m] for m in order])
    live_fields = jnp.stack([fields[m] for m in order])
    last_section = section == sections - 1
    injected_rows = with_fields(dp_spread(injected, parts), live_fields)
    entry_rows = with_fields(
        dp_spread(jnp.concatenate([first, rest]), parts), live_fields
    )
    nothing = jnp.zeros((), BF)
    opening = jnp.where(last_section, injected_rows[:1], entry_rows[:1])
    opening = jnp.where((section == 0) | last_section, opening, nothing)

    def scalars(live, next_idx, ident, add):
        values = [live, next_idx, ident, own, add]
        return jnp.stack([jnp.asarray(v, jnp.int32) for v in values])

    sent = pack_call(
        opening,
        scalars(0, jnp.where(last_section, sections - 1, 0), 0, 0),
        home_cap,
        experts,
        chunk,
        w,
    )
    sent = [b[0] for b in sent]
    bufs = [sent[0]] + [
        lax.ppermute(
            sent[k], JOINT, joint_pairs([(0, 0), (sections - 1, sections - 1)], experts, k)
        )
        for k in range(1, experts)
    ]

    first_held = load_call(w_first, width, sent[0])
    ring = [(s, (s + 1) % sections) for s in range(sections)]
    span = sections * RECUR
    total_steps = span + sections - 1
    finals = {}
    ahead = []
    for t in range(total_steps):
        if t < micro - 1:
            entering = jnp.where(last_section, entry_rows[t + 1], nothing)
            fill = last_section
            ahead.append(list(bufs))
            if t < sections - 2:
                entering = jnp.where(section == sections - 2, injected_rows[t + 1], entering)
                fill = fill | (section == sections - 2)
            at = 0
            for k, buf in enumerate(bufs):
                n = buf.shape[0]
                part = entering[at : at + n]
                part = jnp.pad(part, ((0, n - part.shape[0]), (0, 0)))
                bufs[k] = jnp.where(fill, part, buf)
                at += n
        if t == 1:
            bufs, late, crowded = lax.optimization_barrier((bufs, late, crowded))
        offset = t - section
        live = (offset >= 0) & (offset < span)
        round_of = jnp.clip(offset, 0, span - 1) // sections
        next_idx = jnp.where(live, round_of * sections + section + 1, 0)
        if t < sections - 2:
            next_idx = jnp.where(section == sections - 2, sections - 1, next_idx)
        partial = up_call(bufs, gain, router_row, mask, first_held)
        second_held = load_call(w_second, width, partial)
        partials = dp_partials(partial, parts)
        adding = sections - 1 <= t < 2 * sections - 1
        is_last = t == total_steps - 1
        ident = (section == 0) & (t >= span)
        outs = down_call(
            bufs,
            partials,
            mask,
            second_held,
            scalars(live, next_idx, ident, last_section & adding),
            (ahead + [late])[t - sections + 1] if adding else [],
            [home_cap] * experts if is_last else sizes,
            true_width,
            w,
        )
        if t == 0:
            outs, late_rows, all_routes = lax.optimization_barrier(
                (outs, injected_rows[micro - 1 :], all_routes)
            )
            other, same = pair_counts(all_routes, experts)
            overflow = (jnp.max(other) > other_cap + spare_cap) | (jnp.max(same) > same_cap)
            crowded = jnp.max(jnp.where(when, other[None], 0.0), axis=(1, 2)) > other_cap
            late = pack_call(
                late_rows, scalars(0, sections - 1, 0, 0), home_cap, experts, chunk, w
            )
            late = move([b[0] for b in late], [(1, sections - 1)], experts)
        if is_last:
            finals[sections - 1] = move_within(outs, sections - 1, experts)
        elif t < span:
            bufs, first_held = move_spare(
                outs, crowded[t] if t else None, ring, experts, w_first, width
            )
        else:
            j = t - (sections - 1) - sections
            target = order[j]
            moves = [(s, s + 1) for s in range(t - span + 1, sections - 1)]
            moves.append((sections - 1, target))
            passing = (0, 0) if t < total_steps - 2 else (0, order[0])
            bufs, first_held = move_spare(
                outs, crowded[t], moves, experts, w_first, width, [passing]
            )
            finals[target] = bufs[:experts]
            if t == total_steps - 2:
                finals[order[0]] = bufs[:experts]

    groups = [finals[1], finals[0], finals[sections - 1]]
    which = jnp.where(section == 1, 0, jnp.where(last_section, 2, 1)).astype(jnp.int32)
    rows = unpack_call(groups, which.reshape(1), home, chunk, w)
    result = dp_return(rows[:, :w], parts)
    return result[None], overflow


def body(*arguments):
    result, overflow = direct_body(*arguments)
    return lax.cond(overflow, lambda: general_body(*arguments), lambda: result)


def solution(mesh):
    return jax.shard_map(
        body,
        mesh=mesh,
        in_specs=(
            P(None, ("dp", "expert"), None),
            P(None, ("dp", "expert"), None),
            P(None, "section", None, ("dp", "expert"), None),
            P("section", None),
            P("section", None, None),
            P("section", "expert", "dp", None),
            P("section", "expert", None, "dp"),
        ),
        out_specs=P("section", ("dp", "expert"), None),
        check_vma=False,
    )
```

```python
import functools
import jax
import jax.numpy as jnp
import numpy as np
from jax import lax
from jax.experimental import pallas as pl
from jax.experimental.pallas import tpu as pltpu
from jax.sharding import PartitionSpec as P

RECUR = 2
CAP = 12
SAME_CAP = 20
OTHER_CAP = 16
SPARE_CAP = 4
META = 16
HOME = 8
EPS = 1e-05
VMEM_LIMIT = 16 << 20
BF = jnp.bfloat16
F32 = jnp.float32
JOINT = ("section", "expert")


def shifted(block, axis, distance):
    devices = range(lax.axis_size(axis))
    route = [((i - distance) % len(devices), i) for i in devices]
    return lax.ppermute(block, axis, route)


def normalize(current, gain_row):
    as_float = current.astype(F32)
    inv_rms = lax.rsqrt(jnp.mean(as_float * as_float, axis=-1, keepdims=True) + EPS)
    return (as_float * inv_rms * gain_row).astype(BF)


def expert_rows(item_rows, w_first, w_second):
    extent = item_rows.shape
    flat_rows = item_rows.reshape(-1, extent[-1])
    hidden = jax.nn.gelu(jnp.dot(flat_rows, w_first, preferred_element_type=F32)).astype(BF)
    result = jnp.dot(hidden, w_second, preferred_element_type=F32).astype(BF)
    return result.reshape(extent)


def whole_round(buffer, w_first, w_second):
    processed = expert_rows(
        lax.all_to_all(buffer, "expert", split_axis=0, concat_axis=0, tiled=True), w_first, w_second
    )
    return lax.all_to_all(processed, "expert", split_axis=0, concat_axis=0, tiled=True)


def core_block(current, gain_row, router_rows, w_first, w_second, assign):
    tokens = current.shape[0]
    experts = router_rows.shape[0]
    normed = normalize(current, gain_row)
    logits = jnp.dot(normed, router_rows.T, preferred_element_type=F32)
    labels = lax.broadcasted_iota(jnp.int32, (tokens, experts), 1)
    onehot = (assign[:, None] == labels).astype(F32)
    gate_value = jax.nn.sigmoid(jnp.sum(onehot * logits, axis=-1))
    earlier = (
        lax.broadcasted_iota(jnp.int32, (tokens, tokens), 0)
        > lax.broadcasted_iota(jnp.int32, (tokens, tokens), 1)
    ).astype(F32)
    counts = jnp.dot(earlier, onehot, preferred_element_type=F32)
    slot_index = jnp.sum(onehot * counts, axis=-1).astype(jnp.int32)
    target = assign * CAP + slot_index
    places = (
        lax.broadcasted_iota(jnp.int32, (experts * CAP, tokens), 0) == target[None, :]
    ).astype(BF)
    buffer = (
        jnp.dot(places, normed, preferred_element_type=F32).astype(BF).reshape(experts, CAP, -1)
    )
    returned = whole_round(buffer, w_first, w_second)
    flat_back = returned.reshape(experts * CAP, -1)
    expert_out = jnp.einsum("st,sd->td", places, flat_back, preferred_element_type=F32)
    updated = current.astype(F32) + gate_value[:, None] * expert_out
    return updated.astype(BF)


def general_body(init_state, inject, routes, norm_gain, router, w_up, w_down):
    sections = lax.axis_size("section")
    section_index = lax.axis_index("section")
    w_first = lax.all_gather(w_up, "dp", axis=2, tiled=True)[0, 0]
    w_second = lax.all_gather(w_down, "dp", axis=3, tiled=True)[0, 0]
    gain_row = norm_gain[0]
    router_rows = router[0]
    tokens = init_state.shape[1]
    active_span = sections * RECUR
    total_steps = active_span + sections - 1

    def advance(moment, hidden_state):
        offset = moment - section_index
        is_live = (offset >= 0) & (offset < active_span)
        clipped = jnp.clip(offset, 0, active_span - 1)
        loop_round = clipped // sections
        entry_slot = clipped % sections
        micro_idx = jnp.mod(sections - 2 - entry_slot, sections)
        initial = lax.dynamic_index_in_dim(init_state, micro_idx, 0, keepdims=False)
        injected_row = lax.dynamic_index_in_dim(inject, micro_idx, 0, keepdims=False)
        incoming = jnp.where(loop_round == 0, initial, hidden_state)
        injected = (incoming.astype(F32) + injected_row.astype(F32)).astype(BF)
        entering = is_live & (section_index == 0)
        current = jnp.where(entering, injected, hidden_state)
        assign = lax.dynamic_slice(
            routes, (loop_round, 0, micro_idx, 0, 0), (1, 1, 1, tokens, 1)
        ).reshape(tokens)
        result = core_block(current, gain_row, router_rows, w_first, w_second, assign)
        return jnp.where(is_live, result, hidden_state)

    def advance_one(moment, hidden_state):
        return advance(moment, shifted(hidden_state, "section", 1))

    hidden_state = jnp.zeros(init_state.shape[1:], BF)
    hidden_state = advance(0, hidden_state)
    hidden_state = lax.fori_loop(1, total_steps, advance_one, hidden_state)
    return hidden_state[None]


def rows_of(refs):
    return jnp.concatenate([r[...].astype(F32) for r in refs], axis=0)


def column(block, index):
    lanes = lax.broadcasted_iota(jnp.int32, block.shape, 1)
    return jnp.sum(jnp.where(lanes == index, block, 0.0), axis=1, keepdims=True)


def places_of(meta, at, next_idx, own, sizes, experts, ident):
    same, other = sizes[0], sizes[1]
    spare = sizes[experts] // (experts - 1) if len(sizes) > experts else 0
    main = same + (experts - 1) * other
    rows = meta.shape[0]
    dest = column(meta, at + next_idx)
    lanes = lax.broadcasted_iota(jnp.int32, meta.shape, 1)
    onehot = (((lanes + 1).astype(F32) == dest) & (lanes < experts)).astype(F32)
    earlier = (
        lax.broadcasted_iota(jnp.int32, (rows, rows), 0)
        > lax.broadcasted_iota(jnp.int32, (rows, rows), 1)
    ).astype(F32)
    counts = jnp.dot(earlier.astype(BF), onehot.astype(BF), preferred_element_type=F32)
    rank = jnp.sum(onehot * counts, axis=1, keepdims=True).astype(jnp.int32)
    step = dest.astype(jnp.int32) - 1 - own
    step = jnp.where(step < 0, step + experts, step)
    far = step - 1
    slot = jnp.where(rank < other, same + far * other, main + far * spare - other) + rank
    slot = jnp.where(rank < other + spare, slot, -1)
    slot = jnp.where(step > 0, slot, jnp.where(rank < same, rank, -1))
    slot = jnp.where(dest > 0.0, slot, -1)
    if ident is not None:
        slot = jnp.where(ident > 0, lax.broadcasted_iota(jnp.int32, slot.shape, 0), slot)
    lanes_out = lax.broadcasted_iota(jnp.int32, (rows, sum(sizes)), 1)
    return (lanes_out == slot).astype(F32).astype(BF)


def pack(places, rows, outs):
    packed = lax.dot_general(
        places, rows, (((0,), (0,)), ((), ())), preferred_element_type=F32
    )
    at = 0
    for out in outs:
        cap = out.shape[-2]
        out[...] = packed[at : at + cap].astype(BF).reshape(out.shape)
        at += cap


def whole(space=pltpu.VMEM):
    return pl.BlockSpec(memory_space=space)


def spans(width):
    units = width // 128
    pieces = 2 if units >= 8 else 1
    edges = [128 * (units * n // pieces) for n in range(pieces + 1)]
    return list(zip(edges[:-1], edges[1:]))


def load_call(w, rows, after, given):
    features = w.shape[1]

    def kernel(w_ref, _, out_ref, sem):
        part = pl.ds(0, given)
        copy = pltpu.make_async_copy(w_ref.at[part], out_ref.at[part], sem)
        copy.start()
        if given < rows:
            out_ref[given:] = jnp.zeros((rows - given, features), out_ref.dtype)
        copy.wait()

    return pl.pallas_call(
        kernel,
        in_specs=[whole(pl.ANY)] * 2,
        out_specs=whole(),
        out_shape=pltpu.VMEM((rows, features), w.dtype),
        scratch_shapes=[pltpu.SemaphoreType.DMA],
        compiler_params=pltpu.CompilerParams(vmem_limit_bytes=VMEM_LIMIT),
        cost_estimate=pl.CostEstimate(
            flops=0, bytes_accessed=4 * rows * features, transcendentals=0
        ),
        name="load",
    )(w, after)


def up_call(xs, gain, router_row, mask, w):
    count = len(xs)
    width, features = xs[0].shape[1], w.shape[1]
    rows = sum(x.shape[0] for x in xs)

    def kernel(*refs):
        gain_ref, router_ref, mask_ref, w_ref, out_ref, sent_ref = refs[count:]
        x = rows_of(refs[:count])
        kept = x * mask_ref[...]
        scaled = (x * gain_ref[...]).astype(BF)
        squares = jnp.sum(kept * kept, axis=1, keepdims=True)
        logits = jnp.sum(scaled.astype(F32) * router_ref[...], axis=1, keepdims=True)
        lanes = lax.broadcasted_iota(jnp.int32, (rows, 128), 1)
        stats = jnp.where(lanes == 0, squares, jnp.where(lanes == 1, logits, 0.0))
        out_ref[:, features:] = stats
        upper = [v.astype(BF).astype(F32) for v in (squares, logits)]
        split = upper + [squares - upper[0], logits - upper[1]]
        sent = jnp.zeros((rows, 128), F32)
        for n, value in enumerate(split):
            sent = jnp.where(lanes == n, value, sent)
        sent_ref[:, features:] = sent.astype(BF)
        total = jnp.dot(scaled, w_ref[...], preferred_element_type=F32)
        out_ref[:, :features] = total
        sent_ref[:, :features] = total.astype(BF)

    return pl.pallas_call(
        kernel,
        in_specs=[whole()] * (count + 3) + [whole()],
        out_specs=[whole()] * 2,
        out_shape=[jax.ShapeDtypeStruct((rows, features + 128), t) for t in (F32, BF)],
        compiler_params=pltpu.CompilerParams(vmem_limit_bytes=VMEM_LIMIT),
        cost_estimate=pl.CostEstimate(
            flops=2 * rows * width * features,
            bytes_accessed=2 * rows * width + 4 * rows * features,
            transcendentals=0,
        ),
        name="up",
    )(*xs, gain, router_row, mask, w)


def down_call(xs, partials, mask, w, w_rest, scalars, injected, sizes, true_width, width_local):
    experts = lax.axis_size("expert")
    count, parts = len(xs), len(partials)
    width, features = xs[0].shape[1], w.shape[1]
    rows = sum(x.shape[0] for x in xs)
    pieces = spans(width)
    ready, given = pieces[0][1], w_rest.shape[0]
    streams = ready < width
    at = width_local - (width - 128)
    last = slice(width - 128, width)

    def kernel(*refs):
        refs = list(refs)
        scalar_ref = refs.pop(0)
        x_refs = [refs.pop(0) for _ in range(count)]
        part_refs = [refs.pop(0) for _ in range(parts)]
        mask_ref, w_ref = refs.pop(0), refs.pop(0)
        inj_refs = [refs.pop(0) for _ in injected]
        rest_ref = refs.pop(0)
        if streams:
            held, sem = refs.pop(-2), refs.pop(-1)
            copy = pltpu.make_async_copy(
                rest_ref.at[pl.ds(ready, given - ready)], held.at[pl.ds(0, given - ready)], sem
            )
            copy.start()
            if given < width:
                held[given - ready :] = jnp.zeros((width - given, features), BF)
        out_refs = refs

        total = part_refs[0][...]
        for other in part_refs[1:]:
            total = total + other[...].astype(F32)
        squares, logits = (
            total[:, features + n : features + n + 1] + total[:, features + n + 2 : features + n + 3]
            for n in range(2)
        )
        inv_rms = lax.rsqrt(squares / true_width + EPS)
        gate = jax.nn.sigmoid(logits * inv_rms)
        hidden = jax.nn.gelu(total[:, :features] * inv_rms).astype(BF)
        meta = jnp.concatenate([r[:, last].astype(F32) for r in x_refs], axis=0)
        ident = scalar_ref[2] if rows == sum(sizes) else None
        places = places_of(meta, at, scalar_ref[1], scalar_ref[3], sizes, experts, ident)
        if inj_refs:
            theirs = jnp.concatenate([r[:, last].astype(F32) for r in inj_refs], axis=0)
            which = lax.broadcasted_iota(jnp.int32, (8, 128), 0)
            lane = lax.broadcasted_iota(jnp.int32, (8, 128), 1)
            picks = ((lane == at + HOME + which) & (which < 3)).astype(F32).astype(BF)
            keys = lax.dot_general(
                picks, theirs.astype(BF), (((1,), (1,)), ((), ())), preferred_element_type=F32
            )
            home, low, high = (column(meta, at + HOME + n) for n in range(3))
            same = (home == keys[0:1]) & (low == keys[1:2]) & (high == keys[2:3])
            same = same & (home > 0.0) & (scalar_ref[4] > 0)
            match = same.astype(F32).astype(BF)

        for start, stop in pieces:
            cols = slice(start, stop)
            if start == 0:
                weights = w_ref[...]
            else:
                copy.wait()
                weights = held[...]
            x = jnp.concatenate([r[:, cols].astype(F32) for r in x_refs], axis=0)
            out = lax.dot_general(
                hidden, weights, (((1,), (1,)), ((), ())), preferred_element_type=F32
            ).astype(BF)
            updated = (x + gate * out.astype(F32)).astype(BF)
            state = jnp.where(scalar_ref[0] > 0, updated.astype(F32), x)
            if inj_refs:
                theirs = jnp.concatenate([r[:, cols].astype(F32) for r in inj_refs], axis=0)
                added = jnp.dot(match, theirs.astype(BF), preferred_element_type=F32)
                state = state + added * mask_ref[:, cols]
            packed = lax.dot_general(
                places, state.astype(BF), (((0,), (0,)), ((), ())), preferred_element_type=F32
            )
            row = 0
            for out_ref, n in zip(out_refs, sizes):
                out_ref[:, cols] = packed[row : row + n].astype(BF)
                row += n

    return pl.pallas_call(
        kernel,
        in_specs=[whole(pltpu.SMEM)]
        + [whole()] * (count + parts + 2 + len(injected))
        + [whole(pl.ANY)],
        out_specs=[whole()] * len(sizes),
        scratch_shapes=[pltpu.VMEM((width - ready, features), BF), pltpu.SemaphoreType.DMA]
        if streams
        else [],
        out_shape=[jax.ShapeDtypeStruct((n, width), BF) for n in sizes],
        compiler_params=pltpu.CompilerParams(vmem_limit_bytes=VMEM_LIMIT + (4 << 20)),
        cost_estimate=pl.CostEstimate(
            flops=2 * rows * width * (features + sum(sizes)),
            bytes_accessed=4 * rows * width + 8 * rows * features,
            transcendentals=rows * features,
        ),
        name="down",
    )(scalars, *xs, *partials, mask, w, *injected, w_rest)


def pack_call(rows_in, scalars, out_cap, experts, chunk, width_local):
    batches, rows, width = rows_in.shape
    at = width_local - (width - 128)
    last = width // 128 - 1

    def kernel(scalar_ref, x_ref, meta_ref, *refs):
        out_refs, places_ref = refs[:experts], refs[experts]

        @pl.when(pl.program_id(1) == 0)
        def _():
            meta = meta_ref[0].astype(F32)
            places_ref[...] = places_of(
                meta, at, scalar_ref[1], scalar_ref[3], [out_cap] * experts, experts, None
            )

        pack(places_ref[...], x_ref[0], out_refs)

    return pl.pallas_call(
        kernel,
        grid_spec=pltpu.PrefetchScalarGridSpec(
            num_scalar_prefetch=1,
            grid=(batches, width // chunk),
            in_specs=[
                pl.BlockSpec((1, rows, chunk), lambda j, c, s: (j, 0, c)),
                pl.BlockSpec((1, rows, 128), lambda j, c, s: (j, 0, last)),
            ],
            out_specs=[pl.BlockSpec((1, out_cap, chunk), lambda j, c, s: (j, 0, c))] * experts,
            scratch_shapes=[pltpu.VMEM((rows, experts * out_cap), BF)],
        ),
        out_shape=[jax.ShapeDtypeStruct((batches, out_cap, width), BF)] * experts,
        compiler_params=pltpu.CompilerParams(vmem_limit_bytes=VMEM_LIMIT),
        cost_estimate=pl.CostEstimate(
            flops=2 * batches * rows * width * experts * out_cap,
            bytes_accessed=4 * batches * rows * width,
            transcendentals=0,
        ),
        name="pack",
    )(scalars, rows_in, rows_in)


def unpack_call(groups, which, home_rows, chunk, width_local):
    width = groups[0][0].shape[1]
    at = width_local - (width - 128)
    last = width // 128 - 1
    flat = [b for g in groups for b in g]
    sizes = [len(g) for g in groups]
    totals = [sum(b.shape[0] for b in g) for g in groups]

    def kernel(scalar_ref, *refs):
        refs = list(refs)
        data = [[refs.pop(0) for _ in range(n)] for n in sizes]
        metas = [[refs.pop(0) for _ in range(n)] for n in sizes]
        out_ref = refs.pop(0)

        @pl.when(pl.program_id(0) == 0)
        def _():
            for g, ref in enumerate(refs):
                meta = rows_of(metas[g])
                low, high = column(meta, at + HOME + 1), column(meta, at + HOME + 2)
                token = (high * 128.0 + low).astype(jnp.int32) - 1
                lanes = lax.broadcasted_iota(jnp.int32, ref.shape, 1)
                hit = (lanes == token) & (scalar_ref[0] == g)
                ref[...] = hit.astype(F32).astype(BF)

        total = jnp.zeros(out_ref.shape, F32)
        for g, ref in enumerate(refs):
            total += lax.dot_general(
                ref[...],
                rows_of(data[g]).astype(BF),
                (((0,), (0,)), ((), ())),
                preferred_element_type=F32,
            )
        out_ref[...] = total.astype(BF)

    return pl.pallas_call(
        kernel,
        grid_spec=pltpu.PrefetchScalarGridSpec(
            num_scalar_prefetch=1,
            grid=(width // chunk,),
            in_specs=[pl.BlockSpec((b.shape[0], chunk), lambda c, s: (0, c)) for b in flat]
            + [pl.BlockSpec((b.shape[0], 128), lambda c, s: (0, last)) for b in flat],
            out_specs=pl.BlockSpec((home_rows, chunk), lambda c, s: (0, c)),
            scratch_shapes=[pltpu.VMEM((t, home_rows), BF) for t in totals],
        ),
        out_shape=jax.ShapeDtypeStruct((home_rows, width), BF),
        compiler_params=pltpu.CompilerParams(vmem_limit_bytes=VMEM_LIMIT),
        cost_estimate=pl.CostEstimate(
            flops=2 * sum(totals) * home_rows * width,
            bytes_accessed=2 * sum(totals) * width,
            transcendentals=0,
        ),
        name="unpack",
    )(which, *flat, *flat)


def dp_spread(rows, parts):
    lead, tokens, width = rows.shape
    w = width // parts
    me = lax.axis_index("dp")
    if parts == 2:
        low, high = rows[..., :w], rows[..., w:]
        mine = jnp.where(me == 0, low, high)
        theirs = lax.ppermute(jnp.where(me == 0, high, low), "dp", [(0, 1), (1, 0)])
        first = jnp.where(me == 0, mine, theirs)
        second = jnp.where(me == 0, theirs, mine)
        return jnp.concatenate([first, second], axis=1)
    split = rows.reshape(lead, tokens, parts, w).transpose(2, 0, 1, 3)
    got = lax.all_to_all(split, "dp", 0, 0, tiled=True)
    return got.transpose(1, 0, 2, 3).reshape(lead, parts * tokens, w)


def dp_return(rows, parts):
    tokens, w = rows.shape[0] // parts, rows.shape[1]
    me = lax.axis_index("dp")
    if parts == 2:
        low, high = rows[:tokens], rows[tokens:]
        mine = jnp.where(me == 0, low, high)
        theirs = lax.ppermute(jnp.where(me == 0, high, low), "dp", [(0, 1), (1, 0)])
        return jnp.where(
            me == 0,
            jnp.concatenate([mine, theirs], axis=1),
            jnp.concatenate([theirs, mine], axis=1),
        )
    got = lax.all_to_all(rows.reshape(parts, tokens, w), "dp", 0, 0, tiled=True)
    return got.transpose(1, 0, 2).reshape(tokens, parts * w)


def dp_partials(partial, rounded, parts):
    if parts == 2:
        return [partial, lax.ppermute(rounded, "dp", [(0, 1), (1, 0)])]
    return [lax.psum(partial, "dp")]


def gathered_routes(routes, sections, parts):
    own = routes[:, 0, :, :, 0]
    me = lax.axis_index("section")
    blocks = lax.broadcasted_iota(jnp.int32, (1, sections, 1, 1), 1)
    every = jnp.zeros(own.shape[:1] + (sections,) + own.shape[1:], jnp.int32)
    for k in range(sections):
        got = own if k == 0 else shifted(own, "section", k)
        every = jnp.where(blocks == jnp.mod(me - k, sections), got[:, None], every)
    every = every.reshape((-1,) + own.shape[1:])
    if parts == 2:
        other = lax.ppermute(every, "dp", [(0, 1), (1, 0)])
        first = lax.axis_index("dp") == 0
        return jnp.concatenate(
            [jnp.where(first, every, other), jnp.where(first, other, every)], axis=-1
        )
    return lax.all_gather(every, "dp", axis=2, tiled=True)


def pair_counts(routes, experts):
    labels = jnp.arange(experts, dtype=jnp.int32)
    onehot = (routes[..., None] == labels).astype(BF)
    counts = jnp.einsum(
        "imta,imtb->imab", onehot[:-1], onehot[1:], preferred_element_type=F32
    )
    total = counts
    for k in range(1, experts):
        total = total + shifted(counts, "expert", k)
    like = (labels[:, None] == labels[None, :])[None, None]
    other = jnp.max(jnp.where(like, 0.0, total), axis=(2, 3))
    same = jnp.max(jnp.where(like, total, 0.0), axis=(2, 3))
    return other, same


def joint_pairs(moves, experts, k):
    return [
        (a * experts + e, b * experts + (e + k) % experts) for a, b in moves for e in range(experts)
    ]


def move(bufs, moves, experts, straight=()):
    kept = joint_pairs(straight, experts, 0)
    return [
        lax.ppermute(buf, JOINT, joint_pairs(moves, experts, k) + kept)
        for k, buf in enumerate(bufs)
    ]


def move_spare(bufs, needed, moves, experts, w, width, straight=()):
    kept = joint_pairs(straight, experts, 0)
    bufs = list(bufs)

    def send(spare):
        n = spare.shape[0] // (experts - 1)
        return jnp.concatenate(
            [
                lax.ppermute(
                    spare[k * n : (k + 1) * n], JOINT, joint_pairs(moves, experts, k + 1) + kept
                )
                for k in range(experts - 1)
            ]
        )

    main = move(bufs[:experts], moves, experts, straight)
    held = load_call(w, width, bufs[0], w.shape[0])
    if needed is None:
        spare = send(bufs[experts])
    else:
        spare = lax.cond(needed, send, lambda spare: spare, bufs[experts])
    return main + [spare], held


def move_within(bufs, section, experts):
    return [bufs[0]] + [
        lax.ppermute(bufs[k], JOINT, joint_pairs([(section, section)], experts, k))
        for k in range(1, experts)
    ]


def direct_body(init_state, inject, routes, norm_gain, router, w_up, w_down):
    sections, parts, experts = (lax.axis_size(a) for a in ("section", "dp", "expert"))
    section, own = lax.axis_index("section"), lax.axis_index("expert")
    micro, tokens, true_width = init_state.shape
    w = true_width // parts
    width = -(-(w + META) // 128) * 128
    chunk = width
    home = parts * tokens
    home_cap = CAP * parts
    same_cap, other_cap, spare_cap = SAME_CAP * parts, OTHER_CAP * parts, SPARE_CAP * parts
    sizes = [same_cap] + [other_cap] * (experts - 1) + [spare_cap * (experts - 1)]
    order = [(sections - 2 - j) % sections for j in range(micro)]
    pad = width - w

    all_routes = gathered_routes(routes, sections, parts)
    position = np.argsort(np.array(order))
    moment = np.arange(all_routes.shape[0] - 1)[:, None] + position[None, :]
    when = np.arange(sections * RECUR + sections - 2)[:, None, None] == moment[None]

    mask = (lax.broadcasted_iota(jnp.int32, (1, width), 1) < w).astype(F32)
    gain = lax.dynamic_slice(norm_gain, (0, lax.axis_index("dp") * w), (1, w))
    gain = jnp.pad(gain, ((0, 0), (0, pad)))
    router_row = lax.dynamic_slice(router, (0, own, lax.axis_index("dp") * w), (1, 1, w))[0]
    router_row = jnp.pad(router_row.astype(F32), ((0, 0), (0, pad)))
    w_first, w_second = w_up[0, 0], w_down[0, 0].T
    if w % 16:
        short = ((0, pad), (0, 0))
        w_first, w_second = jnp.pad(w_first, short), jnp.pad(w_second, short)

    token = lax.broadcasted_iota(jnp.int32, (1, micro, home), 2)
    homes = jnp.broadcast_to(own + 1, token.shape).astype(jnp.int32)
    fields = jnp.concatenate([all_routes + 1, homes, token % 128 + 1, token // 128], axis=0)
    fields = jnp.transpose(fields, (1, 2, 0)).astype(BF)
    fields = jnp.pad(fields, ((0, 0), (0, 0), (0, pad - fields.shape[-1])))

    def with_fields(spread, picked):
        return jnp.concatenate([spread, picked], axis=-1)

    def entry(m):
        return (init_state[m].astype(F32) + inject[m].astype(F32)).astype(BF)

    first = entry(order[0])[None]
    rest = jnp.stack([entry(m) for m in order[1:]])
    injected = jnp.stack([inject[m] for m in order])
    live_fields = jnp.stack([fields[m] for m in order])
    last_section = section == sections - 1
    injected_rows = with_fields(dp_spread(injected, parts), live_fields)
    entry_rows = with_fields(
        dp_spread(jnp.concatenate([first, rest]), parts), live_fields
    )
    nothing = jnp.zeros((), BF)
    opening = jnp.where(last_section, injected_rows[:1], entry_rows[:1])
    opening = jnp.where((section == 0) | last_section, opening, nothing)

    def scalars(live, next_idx, ident, add):
        values = [live, next_idx, ident, own, add]
        return jnp.stack([jnp.asarray(v, jnp.int32) for v in values])

    sent = pack_call(
        opening,
        scalars(0, jnp.where(last_section, sections - 1, 0), 0, 0),
        home_cap,
        experts,
        chunk,
        w,
    )
    sent = [b[0] for b in sent]
    bufs = [sent[0]] + [
        lax.ppermute(
            sent[k], JOINT, joint_pairs([(0, 0), (sections - 1, sections - 1)], experts, k)
        )
        for k in range(1, experts)
    ]

    first_held = load_call(w_first, width, sent[0], w_first.shape[0])
    ring = [(s, (s + 1) % sections) for s in range(sections)]
    span = sections * RECUR
    total_steps = span + sections - 1
    finals = {}
    ahead = []
    for t in range(total_steps):
        if t < micro - 1:
            entering = jnp.where(last_section, entry_rows[t + 1], nothing)
            fill = last_section
            ahead.append(list(bufs))
            if t < sections - 2:
                entering = jnp.where(section == sections - 2, injected_rows[t + 1], entering)
                fill = fill | (section == sections - 2)
            at = 0
            for k, buf in enumerate(bufs):
                n = buf.shape[0]
                part = entering[at : at + n]
                part = jnp.pad(part, ((0, n - part.shape[0]), (0, 0)))
                bufs[k] = jnp.where(fill, part, buf)
                at += n
        if t == 1:
            bufs, late, crowded = lax.optimization_barrier((bufs, late, crowded))
        offset = t - section
        live = (offset >= 0) & (offset < span)
        round_of = jnp.clip(offset, 0, span - 1) // sections
        next_idx = jnp.where(live, round_of * sections + section + 1, 0)
        if t < sections - 2:
            next_idx = jnp.where(section == sections - 2, sections - 1, next_idx)
        partial, rounded = up_call(bufs, gain, router_row, mask, first_held)
        ready = spans(width)[0][1]
        second_held = load_call(w_second, ready, partial, min(ready, w_second.shape[0]))
        partials = dp_partials(partial, rounded, parts)
        adding = sections - 1 <= t < 2 * sections - 1
        is_last = t == total_steps - 1
        ident = (section == 0) & (t >= span)
        outs = down_call(
            bufs,
            partials,
            mask,
            second_held,
            w_second,
            scalars(live, next_idx, ident, last_section & adding),
            (ahead + [late])[t - sections + 1] if adding else [],
            [home_cap] * experts if is_last else sizes,
            true_width,
            w,
        )
        if t == 0:
            outs, late_rows, all_routes = lax.optimization_barrier(
                (outs, injected_rows[micro - 1 :], all_routes)
            )
            other, same = pair_counts(all_routes, experts)
            overflow = (jnp.max(other) > other_cap + spare_cap) | (jnp.max(same) > same_cap)
            crowded = jnp.max(jnp.where(when, other[None], 0.0), axis=(1, 2)) > other_cap
            late = pack_call(
                late_rows, scalars(0, sections - 1, 0, 0), home_cap, experts, chunk, w
            )
            late = move([b[0] for b in late], [(1, sections - 1)], experts)
        if is_last:
            finals[sections - 1] = move_within(outs, sections - 1, experts)
        elif t < span:
            bufs, first_held = move_spare(
                outs, crowded[t] if t else None, ring, experts, w_first, width
            )
        else:
            j = t - (sections - 1) - sections
            target = order[j]
            moves = [(s, s + 1) for s in range(t - span + 1, sections - 1)]
            moves.append((sections - 1, target))
            passing = (0, 0) if t < total_steps - 2 else (0, order[0])
            bufs, first_held = move_spare(
                outs, crowded[t], moves, experts, w_first, width, [passing]
            )
            finals[target] = bufs[:experts]
            if t == total_steps - 2:
                finals[order[0]] = bufs[:experts]

    groups = [finals[1], finals[0], finals[sections - 1]]
    which = jnp.where(section == 1, 0, jnp.where(last_section, 2, 1)).astype(jnp.int32)
    rows = unpack_call(groups, which.reshape(1), home, chunk, w)
    result = dp_return(rows[:, :w], parts)
    return result[None], overflow


def body(*arguments):
    result, overflow = direct_body(*arguments)
    return lax.cond(overflow, lambda: general_body(*arguments), lambda: result)


def solution(mesh):
    return jax.shard_map(
        body,
        mesh=mesh,
        in_specs=(
            P(None, ("dp", "expert"), None),
            P(None, ("dp", "expert"), None),
            P(None, "section", None, ("dp", "expert"), None),
            P("section", None),
            P("section", None, None),
            P("section", "expert", "dp", None),
            P("section", "expert", None, "dp"),
        ),
        out_specs=P("section", ("dp", "expert"), None),
        check_vma=False,
    )
```

```python
import functools
import jax
import jax.numpy as jnp
import numpy as np
from jax import lax
from jax.experimental import pallas as pl
from jax.experimental.pallas import tpu as pltpu
from jax.sharding import PartitionSpec as P

RECUR = 2
CAP = 12
SAME_CAP = 20
OTHER_CAP = 16
SPARE_CAP = 4
META = 16
HOME = 8
EPS = 1e-05
VMEM_LIMIT = 16 << 20
BF = jnp.bfloat16
F32 = jnp.float32
JOINT = ("section", "expert")


def shifted(block, axis, distance):
    devices = range(lax.axis_size(axis))
    route = [((i - distance) % len(devices), i) for i in devices]
    return lax.ppermute(block, axis, route)


def normalize(current, gain_row):
    as_float = current.astype(F32)
    inv_rms = lax.rsqrt(jnp.mean(as_float * as_float, axis=-1, keepdims=True) + EPS)
    return (as_float * inv_rms * gain_row).astype(BF)


def expert_rows(item_rows, w_first, w_second):
    extent = item_rows.shape
    flat_rows = item_rows.reshape(-1, extent[-1])
    hidden = jax.nn.gelu(jnp.dot(flat_rows, w_first, preferred_element_type=F32)).astype(BF)
    result = jnp.dot(hidden, w_second, preferred_element_type=F32).astype(BF)
    return result.reshape(extent)


def whole_round(buffer, w_first, w_second):
    processed = expert_rows(
        lax.all_to_all(buffer, "expert", split_axis=0, concat_axis=0, tiled=True), w_first, w_second
    )
    return lax.all_to_all(processed, "expert", split_axis=0, concat_axis=0, tiled=True)


def core_block(current, gain_row, router_rows, w_first, w_second, assign):
    tokens = current.shape[0]
    experts = router_rows.shape[0]
    normed = normalize(current, gain_row)
    logits = jnp.dot(normed, router_rows.T, preferred_element_type=F32)
    labels = lax.broadcasted_iota(jnp.int32, (tokens, experts), 1)
    onehot = (assign[:, None] == labels).astype(F32)
    gate_value = jax.nn.sigmoid(jnp.sum(onehot * logits, axis=-1))
    earlier = (
        lax.broadcasted_iota(jnp.int32, (tokens, tokens), 0)
        > lax.broadcasted_iota(jnp.int32, (tokens, tokens), 1)
    ).astype(F32)
    counts = jnp.dot(earlier, onehot, preferred_element_type=F32)
    slot_index = jnp.sum(onehot * counts, axis=-1).astype(jnp.int32)
    target = assign * CAP + slot_index
    places = (
        lax.broadcasted_iota(jnp.int32, (experts * CAP, tokens), 0) == target[None, :]
    ).astype(BF)
    buffer = (
        jnp.dot(places, normed, preferred_element_type=F32).astype(BF).reshape(experts, CAP, -1)
    )
    returned = whole_round(buffer, w_first, w_second)
    flat_back = returned.reshape(experts * CAP, -1)
    expert_out = jnp.einsum("st,sd->td", places, flat_back, preferred_element_type=F32)
    updated = current.astype(F32) + gate_value[:, None] * expert_out
    return updated.astype(BF)


def general_body(init_state, inject, routes, norm_gain, router, w_up, w_down):
    sections = lax.axis_size("section")
    section_index = lax.axis_index("section")
    w_first = lax.all_gather(w_up, "dp", axis=2, tiled=True)[0, 0]
    w_second = lax.all_gather(w_down, "dp", axis=3, tiled=True)[0, 0]
    gain_row = norm_gain[0]
    router_rows = router[0]
    tokens = init_state.shape[1]
    active_span = sections * RECUR
    total_steps = active_span + sections - 1

    def advance(moment, hidden_state):
        offset = moment - section_index
        is_live = (offset >= 0) & (offset < active_span)
        clipped = jnp.clip(offset, 0, active_span - 1)
        loop_round = clipped // sections
        entry_slot = clipped % sections
        micro_idx = jnp.mod(sections - 2 - entry_slot, sections)
        initial = lax.dynamic_index_in_dim(init_state, micro_idx, 0, keepdims=False)
        injected_row = lax.dynamic_index_in_dim(inject, micro_idx, 0, keepdims=False)
        incoming = jnp.where(loop_round == 0, initial, hidden_state)
        injected = (incoming.astype(F32) + injected_row.astype(F32)).astype(BF)
        entering = is_live & (section_index == 0)
        current = jnp.where(entering, injected, hidden_state)
        assign = lax.dynamic_slice(
            routes, (loop_round, 0, micro_idx, 0, 0), (1, 1, 1, tokens, 1)
        ).reshape(tokens)
        result = core_block(current, gain_row, router_rows, w_first, w_second, assign)
        return jnp.where(is_live, result, hidden_state)

    def advance_one(moment, hidden_state):
        return advance(moment, shifted(hidden_state, "section", 1))

    hidden_state = jnp.zeros(init_state.shape[1:], BF)
    hidden_state = advance(0, hidden_state)
    hidden_state = lax.fori_loop(1, total_steps, advance_one, hidden_state)
    return hidden_state[None]


def rows_of(refs):
    return jnp.concatenate([r[...].astype(F32) for r in refs], axis=0)


def column(block, index):
    lanes = lax.broadcasted_iota(jnp.int32, block.shape, 1)
    return jnp.sum(jnp.where(lanes == index, block, 0.0), axis=1, keepdims=True)


def places_of(meta, at, next_idx, own, sizes, experts, ident):
    same, other = sizes[0], sizes[1]
    spare = sizes[experts] // (experts - 1) if len(sizes) > experts else 0
    main = same + (experts - 1) * other
    rows = meta.shape[0]
    dest = column(meta, at + next_idx)
    lanes = lax.broadcasted_iota(jnp.int32, meta.shape, 1)
    onehot = (((lanes + 1).astype(F32) == dest) & (lanes < experts)).astype(F32)
    earlier = (
        lax.broadcasted_iota(jnp.int32, (rows, rows), 0)
        > lax.broadcasted_iota(jnp.int32, (rows, rows), 1)
    ).astype(F32)
    counts = jnp.dot(earlier.astype(BF), onehot.astype(BF), preferred_element_type=F32)
    rank = jnp.sum(onehot * counts, axis=1, keepdims=True).astype(jnp.int32)
    step = dest.astype(jnp.int32) - 1 - own
    step = jnp.where(step < 0, step + experts, step)
    far = step - 1
    slot = jnp.where(rank < other, same + far * other, main + far * spare - other) + rank
    slot = jnp.where(rank < other + spare, slot, -1)
    slot = jnp.where(step > 0, slot, jnp.where(rank < same, rank, -1))
    slot = jnp.where(dest > 0.0, slot, -1)
    if ident is not None:
        slot = jnp.where(ident > 0, lax.broadcasted_iota(jnp.int32, slot.shape, 0), slot)
    lanes_out = lax.broadcasted_iota(jnp.int32, (rows, sum(sizes)), 1)
    return (lanes_out == slot).astype(F32).astype(BF)


def pack(places, rows, outs):
    packed = lax.dot_general(
        places, rows, (((0,), (0,)), ((), ())), preferred_element_type=F32
    )
    at = 0
    for out in outs:
        cap = out.shape[-2]
        out[...] = packed[at : at + cap].astype(BF).reshape(out.shape)
        at += cap


def whole(space=pltpu.VMEM):
    return pl.BlockSpec(memory_space=space)


def spans(width):
    units = width // 128
    pieces = 2 if units >= 8 else 1
    edges = [128 * (units * n // pieces) for n in range(pieces + 1)]
    return list(zip(edges[:-1], edges[1:]))


def load_call(w, rows, after):
    given, features = w.shape

    def kernel(w_ref, _, out_ref, sem):
        copy = pltpu.make_async_copy(w_ref, out_ref.at[pl.ds(0, given)], sem)
        copy.start()
        if given < rows:
            out_ref[given:] = jnp.zeros((rows - given, features), out_ref.dtype)
        copy.wait()

    return pl.pallas_call(
        kernel,
        in_specs=[whole(pl.ANY)] * 2,
        out_specs=whole(),
        out_shape=pltpu.VMEM((rows, features), w.dtype),
        scratch_shapes=[pltpu.SemaphoreType.DMA],
        compiler_params=pltpu.CompilerParams(vmem_limit_bytes=VMEM_LIMIT),
        cost_estimate=pl.CostEstimate(
            flops=0, bytes_accessed=4 * rows * features, transcendentals=0
        ),
        name="load",
    )(w, after)


def up_call(xs, gain, router_row, mask, w):
    count = len(xs)
    width, features = xs[0].shape[1], w.shape[1]
    rows = sum(x.shape[0] for x in xs)

    def kernel(*refs):
        gain_ref, router_ref, mask_ref, w_ref, out_ref = refs[count:]
        x = rows_of(refs[:count])
        kept = x * mask_ref[...]
        scaled = (x * gain_ref[...]).astype(BF)
        squares = jnp.sum(kept * kept, axis=1, keepdims=True)
        logits = jnp.sum(scaled.astype(F32) * router_ref[...], axis=1, keepdims=True)
        lanes = lax.broadcasted_iota(jnp.int32, (rows, 128), 1)
        stats = jnp.where(lanes == 0, squares, jnp.where(lanes == 1, logits, 0.0))
        out_ref[:, features:] = stats
        out_ref[:, :features] = jnp.dot(scaled, w_ref[...], preferred_element_type=F32)

    return pl.pallas_call(
        kernel,
        in_specs=[whole()] * (count + 3) + [whole()],
        out_specs=whole(),
        out_shape=jax.ShapeDtypeStruct((rows, features + 128), F32),
        compiler_params=pltpu.CompilerParams(vmem_limit_bytes=VMEM_LIMIT),
        cost_estimate=pl.CostEstimate(
            flops=2 * rows * width * features,
            bytes_accessed=2 * rows * width + 4 * rows * features,
            transcendentals=0,
        ),
        name="up",
    )(*xs, gain, router_row, mask, w)


def down_call(xs, partials, mask, w, scalars, injected, sizes, true_width, width_local):
    experts = lax.axis_size("expert")
    count, parts = len(xs), len(partials)
    width, features = xs[0].shape[1], w.shape[1]
    rows = sum(x.shape[0] for x in xs)
    pieces = spans(width)
    at = width_local - (width - 128)
    last = slice(width - 128, width)

    def kernel(*refs):
        refs = list(refs)
        scalar_ref = refs.pop(0)
        x_refs = [refs.pop(0) for _ in range(count)]
        part_refs = [refs.pop(0) for _ in range(parts)]
        mask_ref, w_ref = refs.pop(0), refs.pop(0)
        inj_refs = [refs.pop(0) for _ in injected]
        out_refs = refs

        total = part_refs[0][...]
        for other in part_refs[1:]:
            total = total + other[...]
        squares = total[:, features : features + 1]
        logits = total[:, features + 1 : features + 2]
        inv_rms = lax.rsqrt(squares / true_width + EPS)
        gate = jax.nn.sigmoid(logits * inv_rms)
        hidden = jax.nn.gelu(total[:, :features] * inv_rms).astype(BF)
        meta = jnp.concatenate([r[:, last].astype(F32) for r in x_refs], axis=0)
        ident = scalar_ref[2] if rows == sum(sizes) else None
        places = places_of(meta, at, scalar_ref[1], scalar_ref[3], sizes, experts, ident)
        if inj_refs:
            theirs = jnp.concatenate([r[:, last].astype(F32) for r in inj_refs], axis=0)
            which = lax.broadcasted_iota(jnp.int32, (8, 128), 0)
            lane = lax.broadcasted_iota(jnp.int32, (8, 128), 1)
            picks = ((lane == at + HOME + which) & (which < 3)).astype(F32).astype(BF)
            keys = lax.dot_general(
                picks, theirs.astype(BF), (((1,), (1,)), ((), ())), preferred_element_type=F32
            )
            home, low, high = (column(meta, at + HOME + n) for n in range(3))
            same = (home == keys[0:1]) & (low == keys[1:2]) & (high == keys[2:3])
            same = same & (home > 0.0) & (scalar_ref[4] > 0)
            match = same.astype(F32).astype(BF)

        for start, stop in pieces:
            cols = slice(start, stop)
            x = jnp.concatenate([r[:, cols].astype(F32) for r in x_refs], axis=0)
            out = lax.dot_general(
                hidden, w_ref[cols, :], (((1,), (1,)), ((), ())), preferred_element_type=F32
            ).astype(BF)
            updated = (x + gate * out.astype(F32)).astype(BF)
            state = jnp.where(scalar_ref[0] > 0, updated.astype(F32), x)
            if inj_refs:
                theirs = jnp.concatenate([r[:, cols].astype(F32) for r in inj_refs], axis=0)
                added = jnp.dot(match, theirs.astype(BF), preferred_element_type=F32)
                state = state + added * mask_ref[:, cols]
            packed = lax.dot_general(
                places, state.astype(BF), (((0,), (0,)), ((), ())), preferred_element_type=F32
            )
            row = 0
            for out_ref, n in zip(out_refs, sizes):
                out_ref[:, cols] = packed[row : row + n].astype(BF)
                row += n

    return pl.pallas_call(
        kernel,
        in_specs=[whole(pltpu.SMEM)]
        + [whole()] * (count + parts + 1)
        + [whole()]
        + [whole()] * len(injected),
        out_specs=[whole()] * len(sizes),
        out_shape=[jax.ShapeDtypeStruct((n, width), BF) for n in sizes],
        compiler_params=pltpu.CompilerParams(vmem_limit_bytes=VMEM_LIMIT),
        cost_estimate=pl.CostEstimate(
            flops=2 * rows * width * (features + sum(sizes)),
            bytes_accessed=4 * rows * width + 8 * rows * features,
            transcendentals=rows * features,
        ),
        name="down",
    )(scalars, *xs, *partials, mask, w, *injected)


def pack_call(rows_in, scalars, out_cap, experts, chunk, width_local):
    batches, rows, width = rows_in.shape
    at = width_local - (width - 128)
    last = width // 128 - 1

    def kernel(scalar_ref, x_ref, meta_ref, *refs):
        out_refs, places_ref = refs[:experts], refs[experts]

        @pl.when(pl.program_id(1) == 0)
        def _():
            meta = meta_ref[0].astype(F32)
            places_ref[...] = places_of(
                meta, at, scalar_ref[1], scalar_ref[3], [out_cap] * experts, experts, None
            )

        pack(places_ref[...], x_ref[0], out_refs)

    return pl.pallas_call(
        kernel,
        grid_spec=pltpu.PrefetchScalarGridSpec(
            num_scalar_prefetch=1,
            grid=(batches, width // chunk),
            in_specs=[
                pl.BlockSpec((1, rows, chunk), lambda j, c, s: (j, 0, c)),
                pl.BlockSpec((1, rows, 128), lambda j, c, s: (j, 0, last)),
            ],
            out_specs=[pl.BlockSpec((1, out_cap, chunk), lambda j, c, s: (j, 0, c))] * experts,
            scratch_shapes=[pltpu.VMEM((rows, experts * out_cap), BF)],
        ),
        out_shape=[jax.ShapeDtypeStruct((batches, out_cap, width), BF)] * experts,
        compiler_params=pltpu.CompilerParams(vmem_limit_bytes=VMEM_LIMIT),
        cost_estimate=pl.CostEstimate(
            flops=2 * batches * rows * width * experts * out_cap,
            bytes_accessed=4 * batches * rows * width,
            transcendentals=0,
        ),
        name="pack",
    )(scalars, rows_in, rows_in)


def unpack_call(groups, which, home_rows, chunk, width_local):
    width = groups[0][0].shape[1]
    at = width_local - (width - 128)
    last = width // 128 - 1
    flat = [b for g in groups for b in g]
    sizes = [len(g) for g in groups]
    totals = [sum(b.shape[0] for b in g) for g in groups]

    def kernel(scalar_ref, *refs):
        refs = list(refs)
        data = [[refs.pop(0) for _ in range(n)] for n in sizes]
        metas = [[refs.pop(0) for _ in range(n)] for n in sizes]
        out_ref = refs.pop(0)

        @pl.when(pl.program_id(0) == 0)
        def _():
            for g, ref in enumerate(refs):
                meta = rows_of(metas[g])
                low, high = column(meta, at + HOME + 1), column(meta, at + HOME + 2)
                token = (high * 128.0 + low).astype(jnp.int32) - 1
                lanes = lax.broadcasted_iota(jnp.int32, ref.shape, 1)
                hit = (lanes == token) & (scalar_ref[0] == g)
                ref[...] = hit.astype(F32).astype(BF)

        total = jnp.zeros(out_ref.shape, F32)
        for g, ref in enumerate(refs):
            total += lax.dot_general(
                ref[...],
                rows_of(data[g]).astype(BF),
                (((0,), (0,)), ((), ())),
                preferred_element_type=F32,
            )
        out_ref[...] = total.astype(BF)

    return pl.pallas_call(
        kernel,
        grid_spec=pltpu.PrefetchScalarGridSpec(
            num_scalar_prefetch=1,
            grid=(width // chunk,),
            in_specs=[pl.BlockSpec((b.shape[0], chunk), lambda c, s: (0, c)) for b in flat]
            + [pl.BlockSpec((b.shape[0], 128), lambda c, s: (0, last)) for b in flat],
            out_specs=pl.BlockSpec((home_rows, chunk), lambda c, s: (0, c)),
            scratch_shapes=[pltpu.VMEM((t, home_rows), BF) for t in totals],
        ),
        out_shape=jax.ShapeDtypeStruct((home_rows, width), BF),
        compiler_params=pltpu.CompilerParams(vmem_limit_bytes=VMEM_LIMIT),
        cost_estimate=pl.CostEstimate(
            flops=2 * sum(totals) * home_rows * width,
            bytes_accessed=2 * sum(totals) * width,
            transcendentals=0,
        ),
        name="unpack",
    )(which, *flat, *flat)


def dp_spread(rows, parts):
    lead, tokens, width = rows.shape
    w = width // parts
    me = lax.axis_index("dp")
    if parts == 2:
        low, high = rows[..., :w], rows[..., w:]
        mine = jnp.where(me == 0, low, high)
        theirs = lax.ppermute(jnp.where(me == 0, high, low), "dp", [(0, 1), (1, 0)])
        first = jnp.where(me == 0, mine, theirs)
        second = jnp.where(me == 0, theirs, mine)
        return jnp.concatenate([first, second], axis=1)
    split = rows.reshape(lead, tokens, parts, w).transpose(2, 0, 1, 3)
    got = lax.all_to_all(split, "dp", 0, 0, tiled=True)
    return got.transpose(1, 0, 2, 3).reshape(lead, parts * tokens, w)


def dp_return(rows, parts):
    tokens, w = rows.shape[0] // parts, rows.shape[1]
    me = lax.axis_index("dp")
    if parts == 2:
        low, high = rows[:tokens], rows[tokens:]
        mine = jnp.where(me == 0, low, high)
        theirs = lax.ppermute(jnp.where(me == 0, high, low), "dp", [(0, 1), (1, 0)])
        return jnp.where(
            me == 0,
            jnp.concatenate([mine, theirs], axis=1),
            jnp.concatenate([theirs, mine], axis=1),
        )
    got = lax.all_to_all(rows.reshape(parts, tokens, w), "dp", 0, 0, tiled=True)
    return got.transpose(1, 0, 2).reshape(tokens, parts * w)


def dp_partials(partial, parts):
    if parts == 2:
        return [partial, lax.ppermute(partial, "dp", [(0, 1), (1, 0)])]
    return [lax.psum(partial, "dp")]


def gathered_routes(routes, sections, parts):
    own = routes[:, 0, :, :, 0]
    me = lax.axis_index("section")
    blocks = lax.broadcasted_iota(jnp.int32, (1, sections, 1, 1), 1)
    every = jnp.zeros(own.shape[:1] + (sections,) + own.shape[1:], jnp.int32)
    for k in range(sections):
        got = own if k == 0 else shifted(own, "section", k)
        every = jnp.where(blocks == jnp.mod(me - k, sections), got[:, None], every)
    every = every.reshape((-1,) + own.shape[1:])
    if parts == 2:
        other = lax.ppermute(every, "dp", [(0, 1), (1, 0)])
        first = lax.axis_index("dp") == 0
        return jnp.concatenate(
            [jnp.where(first, every, other), jnp.where(first, other, every)], axis=-1
        )
    return lax.all_gather(every, "dp", axis=2, tiled=True)


def pair_counts(routes, experts):
    labels = jnp.arange(experts, dtype=jnp.int32)
    onehot = (routes[..., None] == labels).astype(BF)
    counts = jnp.einsum(
        "imta,imtb->imab", onehot[:-1], onehot[1:], preferred_element_type=F32
    )
    total = counts
    for k in range(1, experts):
        total = total + shifted(counts, "expert", k)
    like = (labels[:, None] == labels[None, :])[None, None]
    other = jnp.max(jnp.where(like, 0.0, total), axis=(2, 3))
    same = jnp.max(jnp.where(like, total, 0.0), axis=(2, 3))
    return other, same


def joint_pairs(moves, experts, k):
    return [
        (a * experts + e, b * experts + (e + k) % experts) for a, b in moves for e in range(experts)
    ]


def move(bufs, moves, experts, straight=()):
    kept = joint_pairs(straight, experts, 0)
    return [
        lax.ppermute(buf, JOINT, joint_pairs(moves, experts, k) + kept)
        for k, buf in enumerate(bufs)
    ]


def move_spare(bufs, needed, moves, experts, w, width, straight=()):
    kept = joint_pairs(straight, experts, 0)
    bufs = list(bufs)

    def send(spare):
        n = spare.shape[0] // (experts - 1)
        return jnp.concatenate(
            [
                lax.ppermute(
                    spare[k * n : (k + 1) * n], JOINT, joint_pairs(moves, experts, k + 1) + kept
                )
                for k in range(experts - 1)
            ]
        )

    main = move(bufs[:experts], moves, experts, straight)
    held = load_call(w, width, bufs[0])
    if needed is None:
        spare = send(bufs[experts])
    else:
        spare = lax.cond(needed, send, lambda spare: spare, bufs[experts])
    return main + [spare], held


def move_within(bufs, section, experts):
    return [bufs[0]] + [
        lax.ppermute(bufs[k], JOINT, joint_pairs([(section, section)], experts, k))
        for k in range(1, experts)
    ]


def direct_body(init_state, inject, routes, norm_gain, router, w_up, w_down):
    sections, parts, experts = (lax.axis_size(a) for a in ("section", "dp", "expert"))
    section, own = lax.axis_index("section"), lax.axis_index("expert")
    micro, tokens, true_width = init_state.shape
    w = true_width // parts
    width = -(-(w + META) // 128) * 128
    chunk = width
    home = parts * tokens
    home_cap = CAP * parts
    same_cap, other_cap, spare_cap = SAME_CAP * parts, OTHER_CAP * parts, SPARE_CAP * parts
    sizes = [same_cap] + [other_cap] * (experts - 1) + [spare_cap * (experts - 1)]
    order = [(sections - 2 - j) % sections for j in range(micro)]
    pad = width - w

    all_routes = gathered_routes(routes, sections, parts)
    position = np.argsort(np.array(order))
    moment = np.arange(all_routes.shape[0] - 1)[:, None] + position[None, :]
    when = np.arange(sections * RECUR + sections - 2)[:, None, None] == moment[None]

    mask = (lax.broadcasted_iota(jnp.int32, (1, width), 1) < w).astype(F32)
    gain = lax.dynamic_slice(norm_gain, (0, lax.axis_index("dp") * w), (1, w))
    gain = jnp.pad(gain, ((0, 0), (0, pad)))
    router_row = lax.dynamic_slice(router, (0, own, lax.axis_index("dp") * w), (1, 1, w))[0]
    router_row = jnp.pad(router_row.astype(F32), ((0, 0), (0, pad)))
    w_first, w_second = w_up[0, 0], w_down[0, 0].T
    if w % 16:
        short = ((0, pad), (0, 0))
        w_first, w_second = jnp.pad(w_first, short), jnp.pad(w_second, short)

    token = lax.broadcasted_iota(jnp.int32, (1, micro, home), 2)
    homes = jnp.broadcast_to(own + 1, token.shape).astype(jnp.int32)
    fields = jnp.concatenate([all_routes + 1, homes, token % 128 + 1, token // 128], axis=0)
    fields = jnp.transpose(fields, (1, 2, 0)).astype(BF)
    fields = jnp.pad(fields, ((0, 0), (0, 0), (0, pad - fields.shape[-1])))

    def with_fields(spread, picked):
        return jnp.concatenate([spread, picked], axis=-1)

    def entry(m):
        return (init_state[m].astype(F32) + inject[m].astype(F32)).astype(BF)

    first = entry(order[0])[None]
    rest = jnp.stack([entry(m) for m in order[1:]])
    injected = jnp.stack([inject[m] for m in order])
    live_fields = jnp.stack([fields[m] for m in order])
    last_section = section == sections - 1
    injected_rows = with_fields(dp_spread(injected, parts), live_fields)
    entry_rows = with_fields(
        dp_spread(jnp.concatenate([first, rest]), parts), live_fields
    )
    nothing = jnp.zeros((), BF)
    opening = jnp.where(last_section, injected_rows[:1], entry_rows[:1])
    opening = jnp.where((section == 0) | last_section, opening, nothing)

    def scalars(live, next_idx, ident, add):
        values = [live, next_idx, ident, own, add]
        return jnp.stack([jnp.asarray(v, jnp.int32) for v in values])

    sent = pack_call(
        opening,
        scalars(0, jnp.where(last_section, sections - 1, 0), 0, 0),
        home_cap,
        experts,
        chunk,
        w,
    )
    sent = [b[0] for b in sent]
    bufs = [sent[0]] + [
        lax.ppermute(
            sent[k], JOINT, joint_pairs([(0, 0), (sections - 1, sections - 1)], experts, k)
        )
        for k in range(1, experts)
    ]

    first_held = load_call(w_first, width, sent[0])
    ring = [(s, (s + 1) % sections) for s in range(sections)]
    span = sections * RECUR
    total_steps = span + sections - 1
    finals = {}
    ahead = []
    for t in range(total_steps):
        if t < micro - 1:
            entering = jnp.where(last_section, entry_rows[t + 1], nothing)
            fill = last_section
            ahead.append(list(bufs))
            if t < sections - 2:
                entering = jnp.where(section == sections - 2, injected_rows[t + 1], entering)
                fill = fill | (section == sections - 2)
            at = 0
            for k, buf in enumerate(bufs):
                n = buf.shape[0]
                part = entering[at : at + n]
                part = jnp.pad(part, ((0, n - part.shape[0]), (0, 0)))
                bufs[k] = jnp.where(fill, part, buf)
                at += n
        if t == 1:
            bufs, crowded = lax.optimization_barrier((bufs, crowded))
        if t == 2:
            bufs, late = lax.optimization_barrier((bufs, late))
        offset = t - section
        live = (offset >= 0) & (offset < span)
        round_of = jnp.clip(offset, 0, span - 1) // sections
        next_idx = jnp.where(live, round_of * sections + section + 1, 0)
        if t < sections - 2:
            next_idx = jnp.where(section == sections - 2, sections - 1, next_idx)
        partial = up_call(bufs, gain, router_row, mask, first_held)
        second_held = load_call(w_second, width, partial)
        partials = dp_partials(partial, parts)
        adding = sections - 1 <= t < 2 * sections - 1
        is_last = t == total_steps - 1
        ident = (section == 0) & (t >= span)
        outs = down_call(
            bufs,
            partials,
            mask,
            second_held,
            scalars(live, next_idx, ident, last_section & adding),
            (ahead + [late])[t - sections + 1] if adding else [],
            [home_cap] * experts if is_last else sizes,
            true_width,
            w,
        )
        if t == 0:
            outs, late_rows, all_routes = lax.optimization_barrier(
                (outs, injected_rows[micro - 1 :], all_routes)
            )
            other, same = pair_counts(all_routes, experts)
            overflow = (jnp.max(other) > other_cap + spare_cap) | (jnp.max(same) > same_cap)
            crowded = jnp.max(jnp.where(when, other[None], 0.0), axis=(1, 2)) > other_cap
            late = pack_call(
                late_rows, scalars(0, sections - 1, 0, 0), home_cap, experts, chunk, w
            )
            late = move([b[0] for b in late], [(1, sections - 1)], experts)
        if is_last:
            finals[sections - 1] = move_within(outs, sections - 1, experts)
        elif t < span:
            bufs, first_held = move_spare(
                outs, crowded[t] if t else None, ring, experts, w_first, width
            )
        else:
            j = t - (sections - 1) - sections
            target = order[j]
            moves = [(s, s + 1) for s in range(t - span + 1, sections - 1)]
            moves.append((sections - 1, target))
            passing = (0, 0) if t < total_steps - 2 else (0, order[0])
            bufs, first_held = move_spare(
                outs, crowded[t], moves, experts, w_first, width, [passing]
            )
            finals[target] = bufs[:experts]
            if t == total_steps - 2:
                finals[order[0]] = bufs[:experts]

    groups = [finals[1], finals[0], finals[sections - 1]]
    which = jnp.where(section == 1, 0, jnp.where(last_section, 2, 1)).astype(jnp.int32)
    rows = unpack_call(groups, which.reshape(1), home, chunk, w)
    result = dp_return(rows[:, :w], parts)
    return result[None], overflow


def body(*arguments):
    result, overflow = direct_body(*arguments)
    return lax.cond(overflow, lambda: general_body(*arguments), lambda: result)


def solution(mesh):
    return jax.shard_map(
        body,
        mesh=mesh,
        in_specs=(
            P(None, ("dp", "expert"), None),
            P(None, ("dp", "expert"), None),
            P(None, "section", None, ("dp", "expert"), None),
            P("section", None),
            P("section", None, None),
            P("section", "expert", "dp", None),
            P("section", "expert", None, "dp"),
        ),
        out_specs=P("section", ("dp", "expert"), None),
        check_vma=False,
    )
```
